32 devices in a mesh: group: 4 (over y, core), ingroup: 8 (over z, x).
Axes of the slice: x: 2, y: 2, z: 4, core: 2. Of those that a mesh axis runs over, the one named last changes fastest.
Arguments:
- context: bfloat16 [512, 8192], P('group', 'ingroup'), may hold values from -6 to 6
- out_proj: bfloat16 [8192, 7168], P('ingroup'), may hold values from -0.0625 to 0.0625
- residual: bfloat16 [512, 7168], P(('group', 'ingroup')), may hold values from -6 to 6
- norm_gain: float32 [7168], replicated, may hold values from 0.25 to 1.75
- expert_ids: int32 [512, 8], P(('group', 'ingroup')), may hold values from 0 to 7, as said below
- gates: bfloat16 [512, 8], P(('group', 'ingroup')), may hold values from 0.099609375 to 1
- gate_proj: bfloat16 [32, 7168, 256], P(('group', 'ingroup')), may hold values from -0.0625 to 0.0625
- up_proj: bfloat16 [32, 7168, 256], P(('group', 'ingroup')), may hold values from -0.0625 to 0.0625
- down_proj: bfloat16 [32, 256, 7168], P(('group', 'ingroup')), may hold values from -0.1875 to 0.1875
Outputs:
- layer_out: bfloat16 [512, 7168], P(('group', 'ingroup'))
The draws below stay inside these ranges and needn't reach their ends.
Inputs may be any that keep to these rules, and one draw needn't show every extreme that they name: `expert_ids`: each row names 8 different experts, all of them in at most 4 expert groups, expert e lying in group e // 2.
All inputs are finite; a program needn't handle non-finite values.
Results may differ from the reference program's by a relative error of at most 0.012.
Values may be sent and summed in bfloat16 or wider, within the bound.
A program may use at most 128 MiB of HBM per device.

```python
import math
import jax
import jax.numpy as jnp
from jax import lax

D = 7168
HEADS = 64
HEAD_DIM = 128
EXP_HIDDEN = 1024
TOPK = 8
TOPG = 4
SLICES = 4
TOK_DEV = 16
TOKENS = 512
EXPERTS = 8
HID_SLICE = 256
ECAP = 16
N_GROUP = 4
N_INGROUP = 8


def draw_expert_ids(key, part):
    key_bias, key_jitter = jax.random.split(jax.random.fold_in(key, 17))
    favour = jax.random.randint(key_bias, (EXPERTS,), 0, 4) * 300
    jitter = jax.random.randint(key_jitter, (TOKENS, EXPERTS), 0, 1000)
    expert_iota = jnp.arange(EXPERTS, dtype=jnp.int32)
    scores = (favour[None, :] + jitter) * EXPERTS + expert_iota[None, :]
    grouped = scores.reshape(TOKENS, N_GROUP, EXPERTS // N_GROUP)
    best_two = lax.top_k(grouped, 2)[0]
    group_scores = jnp.sum(best_two, axis=2) * N_GROUP + jnp.arange(N_GROUP, dtype=jnp.int32)[None, :]
    top_groups = lax.top_k(group_scores, TOPG)[1]
    allowed = jnp.any(top_groups[:, :, None] == jnp.arange(N_GROUP, dtype=jnp.int32)[None, None, :], axis=1)
    allowed_experts = jnp.repeat(allowed, EXPERTS // N_GROUP, axis=1)
    masked = jnp.where(allowed_experts, scores, -1)
    return lax.top_k(masked, TOPK)[1].astype(jnp.int32)


def block_scale(key, extent, cuts, smallest, top_value):
    loudness = 1.0
    for dim, shards_of in cuts:
        steps = jax.random.uniform(jax.random.fold_in(jax.random.fold_in(key, 6), dim), (shards_of,), jnp.float32, smallest / len(cuts), top_value / len(cuts))
        loudness = loudness * jnp.repeat(jnp.exp(steps), extent[dim] // shards_of).reshape((-1,) + (1,) * (len(extent) - 1 - dim))
    return loudness


def bell_draw(own_key, dims, spread, reach, shards=(), kind=jnp.bfloat16):
    entries = spread * jax.random.normal(own_key, dims, jnp.float32)
    if shards:
        entries = entries * block_scale(own_key, dims, shards, -0.22, 0.18)
    return jnp.clip(entries, -reach, reach).astype(kind)


def setup_inputs(seed: int = 0) -> dict:
    keys = jax.random.split(jax.random.key(seed), 10)
    context = bell_draw(keys[0], (TOKENS, HEADS * HEAD_DIM), 1.0, 6.0, ((0, 4), (1, 8)))
    out_proj = bell_draw(keys[1], (HEADS * HEAD_DIM, D), (HEADS * HEAD_DIM) ** -0.5, 0.0625, ((0, 8),))
    residual = bell_draw(keys[2], (TOKENS, D), 1.0, 6.0, ((0, 32),))
    norm_gain = jnp.clip(1.0 + 0.15 * jax.random.normal(keys[3], (D,), jnp.float32), 0.25, 1.75)
    expert_ids = draw_expert_ids(jax.random.fold_in(keys[9], 71), 0)
    gates = jnp.clip(jnp.exp(math.log(1.0) - 2.306499 * jax.random.uniform(keys[5], (TOKENS, TOPK), jnp.float32) ** block_scale(keys[5], (TOKENS, TOPK), ((0, 32),), -0.2, 0.2)), 0.099609375, 1.0).astype(jnp.bfloat16)
    gate_proj = bell_draw(keys[6], (EXPERTS * SLICES, D, HID_SLICE), D ** -0.5, 0.0625, ((0, 32),))
    up_proj = bell_draw(keys[7], (EXPERTS * SLICES, D, HID_SLICE), D ** -0.5, 0.0625, ((0, 32),))
    down_proj = bell_draw(keys[8], (EXPERTS * SLICES, HID_SLICE, D), EXP_HIDDEN ** -0.5, 0.1875, ((0, 32),))
    return {"context": context, "out_proj": out_proj, "residual": residual, "norm_gain": norm_gain, "expert_ids": expert_ids, "gates": gates, "gate_proj": gate_proj, "up_proj": up_proj, "down_proj": down_proj}


def reference(context, out_proj, residual, norm_gain, expert_ids, gates, gate_proj, up_proj, down_proj):
    attended = jnp.dot(context, out_proj, preferred_element_type=jnp.float32)
    hidden = (residual.astype(jnp.float32) + attended).astype(jnp.bfloat16)
    hidden_wide = hidden.astype(jnp.float32)
    inverse = lax.rsqrt(lax.optimization_barrier(jnp.mean(hidden_wide * hidden_wide, axis=1, keepdims=True)) + 1e-06)
    normed = (hidden_wide * inverse * norm_gain).astype(jnp.bfloat16)
    device_total = N_GROUP * N_INGROUP
    slot_total = device_total * ECAP
    expert_iota = jnp.arange(EXPERTS, dtype=jnp.int32)
    matches = expert_ids[:, :, None] == expert_iota[None, None, :]
    picked = jnp.any(matches, axis=1)
    weighted = lax.optimization_barrier(jnp.sum(jnp.where(matches, gates.astype(jnp.float32)[:, :, None], jnp.float32(0)), axis=1))
    picked_count = picked.astype(jnp.int32)
    by_device = picked_count.reshape(device_total, TOK_DEV, EXPERTS)
    ranking = (jnp.cumsum(by_device, axis=1) - by_device).reshape(TOKENS, EXPERTS)
    admitted = picked & (ranking < ECAP)
    token_iota = jnp.arange(TOKENS, dtype=jnp.int32)
    owner = token_iota // TOK_DEV
    position = jnp.where(admitted, owner[:, None] * ECAP + ranking, slot_total).astype(jnp.int32)
    expert_index = jnp.broadcast_to(expert_iota[None, :], (TOKENS, EXPERTS))
    token_index = jnp.broadcast_to(token_iota[:, None], (TOKENS, EXPERTS))
    slot_tokens = jnp.zeros((EXPERTS, slot_total), jnp.int32).at[expert_index, position].set(token_index, mode='drop')
    filled = jnp.zeros((EXPERTS, slot_total), jnp.float32).at[expert_index, position].set(weighted, mode='drop')

    def one_expert(mixture, expert):
        gathered = jnp.take(normed, slot_tokens[expert], axis=0)
        summed = jnp.zeros((slot_total, D), jnp.float32)
        for slice_index in range(SLICES):
            block_index = expert * SLICES + slice_index
            gate_part = jnp.dot(gathered, gate_proj[block_index], preferred_element_type=jnp.float32)
            up_part = jnp.dot(gathered, up_proj[block_index], preferred_element_type=jnp.float32)
            activated = (jax.nn.silu(gate_part) * up_part).astype(jnp.bfloat16)
            partial_out = jnp.dot(activated, down_proj[block_index], preferred_element_type=jnp.float32).astype(jnp.bfloat16)
            summed = summed + partial_out.astype(jnp.float32)
        mixture = mixture.at[slot_tokens[expert]].add(summed * filled[expert][:, None])
        return (mixture, jnp.int32(0))
    mixture, unused = lax.scan(one_expert, jnp.zeros((TOKENS, D), jnp.float32), expert_iota)
    return (hidden_wide + mixture).astype(jnp.bfloat16)
```

```python
import functools

import jax
import jax.numpy as jnp
from jax import lax
from jax.experimental import pallas as pl
from jax.experimental.pallas import tpu as pltpu
from jax.sharding import PartitionSpec as P

TOPK = 8
SLICES = 4


def slice_output(arrived, gate_block, up_block, down_block):
    shape_in = arrived.shape
    flat_rows = arrived.reshape(-1, shape_in[-1])
    gate_part = jnp.dot(flat_rows, gate_block, preferred_element_type=jnp.float32)
    up_part = jnp.dot(flat_rows, up_block, preferred_element_type=jnp.float32)
    activated = (jax.nn.silu(gate_part) * up_part).astype(jnp.bfloat16)
    partial_out = jnp.dot(activated, down_block, preferred_element_type=jnp.float32).astype(
        jnp.bfloat16
    )
    return partial_out.reshape(shape_in[0], shape_in[1], down_block.shape[1])


def local(context, out_proj, residual, norm_gain, expert_ids, gates, gate_proj, up_proj, down_proj):
    group_count = lax.axis_size("group")
    member_count = lax.axis_size("ingroup")
    rows_here = residual.shape[0]
    model_width = residual.shape[1]
    local_experts = member_count // SLICES
    expert_total = group_count * local_experts
    capacity = min(rows_here, max(2, rows_here * TOPK * 5 // (4 * expert_total)))
    attended = lax.psum_scatter(
        jnp.dot(context, out_proj, preferred_element_type=jnp.float32),
        "ingroup",
        scatter_dimension=0,
        tiled=True,
    )
    hidden = (residual.astype(jnp.float32) + attended).astype(jnp.bfloat16)
    hidden_wide = hidden.astype(jnp.float32)
    inverse = lax.rsqrt(jnp.mean(hidden_wide * hidden_wide, axis=1, keepdims=True) + 1e-06)
    normed = (hidden_wide * inverse * norm_gain).astype(jnp.bfloat16)
    expert_iota = jnp.arange(expert_total, dtype=jnp.int32)
    matches = expert_ids[:, :, None] == expert_iota[None, None, :]
    picked = jnp.any(matches, axis=1)
    weighted = jnp.sum(
        jnp.where(matches, gates.astype(jnp.float32)[:, :, None], jnp.float32(0)), axis=1
    )
    gate_block = gate_proj[0]
    up_block = up_proj[0]
    down_block = down_proj[0]
    capacity_iota = jnp.arange(capacity, dtype=jnp.int32)
    picked_grid = picked.reshape(rows_here, group_count, local_experts)
    touched = jnp.any(picked_grid, axis=2).astype(jnp.int32)
    placed_at = jnp.cumsum(touched, axis=0) - touched
    slot_iota = jnp.arange(rows_here, dtype=jnp.int32)
    selector = (touched.T[:, None, :] > 0) & (placed_at.T[:, None, :] == slot_iota[None, :, None])
    selector_half = selector.astype(jnp.bfloat16)
    outgoing = jnp.einsum(
        "gst,td->gsd", selector_half, normed, preferred_element_type=jnp.float32
    ).astype(jnp.bfloat16)
    gate_grid = weighted.reshape(rows_here, group_count, local_experts).astype(jnp.bfloat16)
    outgoing_gates = jnp.einsum(
        "gst,tgl->gsl", selector_half, gate_grid, preferred_element_type=jnp.float32
    ).astype(jnp.bfloat16)
    arrived_rows, arrived_gates = (
        lax.all_to_all(outgoing, "group", split_axis=0, concat_axis=0, tiled=True),
        lax.all_to_all(outgoing_gates, "group", split_axis=0, concat_axis=0, tiled=True),
    )
    wanted = (arrived_gates > 0).astype(jnp.int32)
    relay_rank = jnp.cumsum(wanted, axis=1) - wanted
    relay_admit = (wanted > 0) & (relay_rank < capacity)
    admit_order = relay_admit.transpose(2, 0, 1)
    rank_order = relay_rank.transpose(2, 0, 1)
    placing = admit_order[:, :, None, :] & (
        rank_order[:, :, None, :] == capacity_iota[None, None, :, None]
    )
    placing_half = placing.astype(jnp.bfloat16)
    expert_rows = jnp.einsum(
        "lgcs,gsd->lgcd", placing_half, arrived_rows, preferred_element_type=jnp.float32
    ).astype(jnp.bfloat16)
    expert_rows = expert_rows.reshape(local_experts, group_count * capacity, model_width)
    dispatch = jnp.broadcast_to(
        expert_rows[:, None], (local_experts, SLICES, group_count * capacity, model_width)
    )
    dispatch = dispatch.reshape(member_count, group_count * capacity, model_width)
    returned = lax.all_to_all(
        slice_output(
            lax.all_to_all(dispatch, "ingroup", split_axis=0, concat_axis=0, tiled=True),
            gate_block,
            up_block,
            down_block,
        ),
        "ingroup",
        split_axis=0,
        concat_axis=0,
        tiled=True,
    )
    returned = returned.reshape(local_experts, SLICES, group_count, capacity, model_width)
    scaled = placing_half * arrived_gates.transpose(2, 0, 1)[:, :, None, :]
    group_out = jnp.einsum("lgcs,lugcd->gsd", scaled, returned, preferred_element_type=jnp.float32)
    back_home = lax.all_to_all(group_out, "group", split_axis=0, concat_axis=0, tiled=True)
    group_iota = jnp.arange(group_count, dtype=jnp.int32)
    fetched = back_home[group_iota[:, None], placed_at.T]
    mixture = jnp.sum(jnp.where(touched.T[:, :, None] > 0, fetched, jnp.float32(0)), axis=0)
    return (hidden_wide + mixture).astype(jnp.bfloat16)


SIDE = 2
DEPTH = 4
CHUNKS = 4
OFFSETS = (0, 1, -1, 2, -2, 3, -3)
MESH = pl.DeviceIdType.MESH
BF16 = jnp.bfloat16
F32 = jnp.float32


class Place:
    def __init__(self):
        group, member = lax.axis_index("group"), lax.axis_index("ingroup")
        self.y, self.c = lax.div(group, 2), lax.rem(group, 2)
        self.z, self.x = lax.div(member, SIDE), lax.rem(member, SIDE)
        self.xo, self.yo, self.co = 1 - self.x, 1 - self.y, 1 - self.c
        self.at_x = {"group": group, "ingroup": self.z * SIDE + self.xo}
        self.at_y = {"group": self.yo * 2 + self.c, "ingroup": member}
        self.at_core = {"group": self.y * 2 + self.co, "ingroup": member}

    def at_z(self, step):
        z = lax.rem(self.z + step + DEPTH, DEPTH)
        return {"group": self.y * 2 + self.c, "ingroup": z * SIDE + self.x}

    def has_z(self, offset):
        return jnp.logical_and(self.z + offset >= 0, self.z + offset < DEPTH)

    def meet(self):
        barrier = pltpu.get_barrier_semaphore()
        for device in (self.at_x, self.at_y, self.at_core, self.at_z(1), self.at_z(-1)):
            pl.semaphore_signal(barrier, inc=1, device_id=device, device_id_type=MESH)
        pl.semaphore_wait(barrier, 5)


def remote(source, target, send, recv, device):
    return pltpu.make_async_remote_copy(
        src_ref=source, dst_ref=target, send_sem=send, recv_sem=recv, device_id=device,
        device_id_type=MESH,
    )


def chain_z(place, sums, slots, send, recv, columns, order=(3, 2, 1)):
    z = place.z
    for k in order:
        for way, step in enumerate((1, -1)):
            @pl.when(place.has_z(step * k))
            def _():
                block = sums.at[z + step * k, :, columns]
                if k < DEPTH - 1:
                    @pl.when(place.has_z(-step))
                    def _():
                        landed = slots.at[way, k, :, columns]
                        remote(landed, landed, send.at[way, k], recv.at[way, k], place.at_z(step)).wait_recv()
                        block[...] = (block[...].astype(F32) + landed[...].astype(F32)).astype(BF16)
                remote(
                    block, slots.at[way, k - 1, :, columns], send.at[way, k - 1], recv.at[way, k - 1],
                    place.at_z(step),
                ).start()


def chain_z_end(place, slots, total, send, recv, columns):
    for way, step in enumerate((1, -1)):
        @pl.when(place.has_z(-step))
        def _():
            landed = slots.at[way, 0, :, columns]
            remote(landed, landed, send.at[way, 0], recv.at[way, 0], place.at_z(step)).wait_recv()
            total[:, columns] += landed[...].astype(F32)


def chain_z_sent(place, sums, slots, send, recv, columns):
    for k in (3, 2, 1):
        for way, step in enumerate((1, -1)):
            @pl.when(place.has_z(step * k))
            def _():
                remote(
                    sums.at[place.z + step * k, :, columns], slots.at[way, k - 1, :, columns],
                    send.at[way, k - 1], recv.at[way, k - 1], place.at_z(step),
                ).wait_send()


def spread_kernel(
    part, residual, gain, hidden, rows_out,
    x_slots, sums, z_slots, total,
    x_send, x_recv, z_send, z_recv,
    a_send, a_recv, b_send, b_recv, d_send, d_recv, c_send, c_recv,
):
    place = Place()
    width = residual.shape[1]
    chunk = width // CHUNKS
    place.meet()
    cuts = [pl.ds(i * chunk, chunk) for i in range(CHUNKS)]

    def x_copy(i):
        return remote(
            part.at[:, place.xo, :, cuts[i]], x_slots.at[:, :, cuts[i]], x_send.at[i], x_recv.at[i],
            place.at_x,
        )

    for i in range(CHUNKS):
        x_copy(i).start()
    for i in range(CHUNKS):
        x_copy(i).wait_recv()
        for d in range(DEPTH):
            sums[d, :, cuts[i]] = (
                part[d, place.x, :, cuts[i]].astype(F32) + x_slots[d, :, cuts[i]].astype(F32)
            ).astype(BF16)
        total[:, cuts[i]] = residual[:, cuts[i]].astype(F32) + sums[place.z, :, cuts[i]].astype(F32)
        chain_z(place, sums, z_slots, z_send.at[i], z_recv.at[i], cuts[i])
    for i in range(CHUNKS):
        chain_z_end(place, z_slots, total, z_send.at[i], z_recv.at[i], cuts[i])
    hidden[...] = total[...].astype(BF16)
    wide = hidden[...].astype(F32)
    inverse = lax.rsqrt(jnp.mean(wide * wide, axis=1, keepdims=True) + 1e-06)

    def index(y, c, z, x):
        return ((y * 2 + c) * DEPTH + z) * SIDE + x

    x, y, z, c = place.x, place.y, place.z, place.c
    half = width // 2
    cut_a, cut_b = pl.ds(0, half), pl.ds(half, half)
    rows_out[index(y, c, z, x)] = (wide * inverse * gain[...]).astype(BF16)

    def here(i, by_x, by_y):
        return index(place.yo if by_y else y, c, z - OFFSETS[i], place.xo if by_x else x)

    def copy_to(device, block, columns, send, recv):
        ref = rows_out.at[block, :, columns]
        return remote(ref, ref, send, recv, device)

    whole = pl.ds(0, width)

    def z_copy(i, step):
        there = OFFSETS.index(OFFSETS[i] + step)
        return copy_to(
            place.at_z(step), here(i, False, False), whole, a_send.at[there], a_recv.at[there]
        )

    def z_steps(i):
        offset = OFFSETS[i]
        return [s for s in (1, -1) if offset * s >= 0 and abs(offset + s) < DEPTH]

    def x_full(i):
        return copy_to(place.at_x, here(i, False, False), whole, b_send.at[i, 0], b_recv.at[i, 0])

    def y_full(i):
        return copy_to(place.at_y, here(i, False, False), whole, b_send.at[i, 1], b_recv.at[i, 1])

    def y_half(i):
        return copy_to(place.at_y, here(i, True, False), cut_a, d_send.at[i, 0], d_recv.at[i, 0])

    def x_half(i):
        return copy_to(place.at_x, here(i, False, True), cut_b, d_send.at[i, 1], d_recv.at[i, 1])

    def core_copy(i, by_x, by_y):
        k = by_x * 2 + by_y
        return copy_to(
            place.at_core, here(i, by_x, by_y), whole, c_send.at[i, k], c_recv.at[i, k]
        )

    def along_z(i):
        @pl.when(place.has_z(-OFFSETS[i]))
        def _():
            if i > 0:
                copy_to(place.at_x, here(i, False, False), whole, a_send.at[i], a_recv.at[i]).wait_recv()
            for step in z_steps(i):
                @pl.when(place.has_z(step))
                def _():
                    z_copy(i, step).start()
            x_full(i).start()
            y_full(i).start()
            core_copy(i, 0, 0).start()

    def along_xy(i):
        @pl.when(place.has_z(-OFFSETS[i]))
        def _():
            copy_to(place.at_x, here(i, True, False), whole, b_send.at[i, 0], b_recv.at[i, 0]).wait_recv()
            y_half(i).start()
            core_copy(i, 1, 0).start()
            copy_to(place.at_x, here(i, False, True), whole, b_send.at[i, 1], b_recv.at[i, 1]).wait_recv()
            x_half(i).start()
            core_copy(i, 0, 1).start()

    def along_diagonal(i):
        @pl.when(place.has_z(-OFFSETS[i]))
        def _():
            for k, columns in enumerate((cut_a, cut_b)):
                copy_to(
                    place.at_x, here(i, True, True), columns, d_send.at[i, k], d_recv.at[i, k]
                ).wait_recv()
            core_copy(i, 1, 1).start()

    near = ((0,), (1, 2), (3, 4), (5, 6))
    for t in range(DEPTH + 2):
        for i in near[t] if t < DEPTH else ():
            along_z(i)
        for i in near[t - 1] if 0 <= t - 1 < DEPTH else ():
            along_xy(i)
        for i in near[t - 2] if 0 <= t - 2 < DEPTH else ():
            along_diagonal(i)
    for i in range(len(OFFSETS)):
        @pl.when(place.has_z(-OFFSETS[i]))
        def _():
            for step in z_steps(i):
                @pl.when(place.has_z(step))
                def _():
                    z_copy(i, step).wait_send()
            for copy in (x_full(i), y_full(i), x_half(i), y_half(i)):
                copy.wait_send()
            for by_x in (0, 1):
                for by_y in (0, 1):
                    core_copy(i, by_x, by_y).wait_send()
                    block = index(
                        place.yo if by_y else y, place.co, z - OFFSETS[i], place.xo if by_x else x
                    )
                    copy_to(
                        place.at_core, block, whole, c_send.at[i, by_x * 2 + by_y],
                        c_recv.at[i, by_x * 2 + by_y],
                    ).wait_recv()
    for i in range(CHUNKS):
        x_copy(i).wait_send()
        chain_z_sent(place, sums, z_slots, z_send.at[i], z_recv.at[i], cuts[i])


def gather_sum_kernel(
    parts, mixture,
    core_slots, sums, a_slots, b_slots, x_slots, y_slots, own, z_slots,
    c_send, c_recv, d_send, d_recv, f_send, f_recv, z_send, z_recv,
):
    place = Place()
    width = mixture.shape[1]
    half = width // 2
    cut_a, cut_b, whole = pl.ds(0, half), pl.ds(half, half), pl.ds(0, width)
    x, y, z, xo, yo = place.x, place.y, place.z, place.xo, place.yo
    place.meet()
    far = (6, 5, 4, 3, 2, 1, 0)

    def core_copy(i):
        d = z - OFFSETS[i]
        return remote(
            parts.at[:, place.co, d], core_slots.at[d], c_send.at[i], c_recv.at[i], place.at_core
        )

    def diagonal_a(i):
        d = z - OFFSETS[i]
        return remote(
            sums.at[d, yo, xo, :, cut_a], a_slots.at[d], d_send.at[i, 0], d_recv.at[i, 0], place.at_y
        )

    def diagonal_b(i):
        d = z - OFFSETS[i]
        return remote(
            sums.at[d, yo, xo, :, cut_b], b_slots.at[d], d_send.at[i, 1], d_recv.at[i, 1], place.at_x
        )

    def full_x(i):
        d = z - OFFSETS[i]
        return remote(sums.at[d, y, xo], x_slots.at[d], f_send.at[i, 0], f_recv.at[i, 0], place.at_x)

    def full_y(i):
        d = z - OFFSETS[i]
        return remote(sums.at[d, yo, x], y_slots.at[d], f_send.at[i, 1], f_recv.at[i, 1], place.at_y)

    def each(i, body):
        pl.when(place.has_z(-OFFSETS[i]))(body)

    def first(i):
        def body():
            d = z - OFFSETS[i]
            core_copy(i).wait_recv()
            for j in (yo, y):
                for k in (xo, x):
                    sums[d, j, k] = (
                        parts[j, place.c, d, k].astype(F32) + core_slots[d, j, k].astype(F32)
                    ).astype(BF16)
                if j is yo:
                    diagonal_a(i).start()
                    diagonal_b(i).start()

        each(i, body)

    def second(i):
        def body():
            d = z - OFFSETS[i]
            diagonal_a(i).wait_recv()
            sums[d, y, xo, :, cut_a] = (
                sums[d, y, xo, :, cut_a].astype(F32) + a_slots[d].astype(F32)
            ).astype(BF16)
            full_x(i).start()
            diagonal_b(i).wait_recv()
            sums[d, yo, x, :, cut_b] = (
                sums[d, yo, x, :, cut_b].astype(F32) + b_slots[d].astype(F32)
            ).astype(BF16)
            full_y(i).start()

        each(i, body)

    def third(i):
        def body():
            d = z - OFFSETS[i]
            full_x(i).wait_recv()
            full_y(i).wait_recv()
            own[d] = (
                sums[d, y, x].astype(F32) + x_slots[d].astype(F32) + y_slots[d].astype(F32)
            ).astype(BF16)

        each(i, body)

    levels = ((6, 5), (4, 3), (2, 1), (0,))
    for i in far:
        each(i, lambda i=i: core_copy(i).start())
    for t in range(len(levels) + 2):
        for i in levels[t] if t < len(levels) else ():
            first(i)
        for i in levels[t - 1] if 0 <= t - 1 < len(levels) else ():
            second(i)
        if 0 <= t - 2 < len(levels):
            for i in levels[t - 2]:
                third(i)
            if t - 2 < DEPTH - 1:
                chain_z(place, own, z_slots, z_send, z_recv, whole, order=(DEPTH - 1 - (t - 2),))
    mixture[...] = own[z].astype(F32)
    chain_z_end(place, z_slots, mixture, z_send, z_recv, whole)
    for i in far:
        def body(i=i):
            for copy in (core_copy(i), diagonal_a(i), diagonal_b(i), full_x(i), full_y(i)):
                copy.wait_send()

        each(i, body)
    chain_z_sent(place, own, z_slots, z_send, z_recv, whole)


def local_dense(
    context, out_proj, residual, norm_gain, expert_ids, gates, gate_proj, up_proj, down_proj
):
    group_count = lax.axis_size("group")
    member_count = lax.axis_size("ingroup")
    devices = group_count * member_count
    rows, width = residual.shape
    local_experts = member_count // SLICES
    expert_total = group_count * local_experts
    capacity = min(rows, max(2, rows * TOPK * 5 // (4 * expert_total)))
    offsets = len(OFFSETS)
    dma = pltpu.SemaphoreType.DMA
    vmem = pl.BlockSpec(memory_space=pltpu.VMEM)

    matches = expert_ids[:, :, None] == jnp.arange(expert_total, dtype=jnp.int32)[None, None, :]
    picked = jnp.any(matches, axis=1).astype(jnp.int32)
    ranking = jnp.cumsum(picked, axis=0) - picked
    weighted = jnp.sum(jnp.where(matches, gates.astype(F32)[:, :, None], F32(0)), axis=1)
    weighted = jnp.where((picked > 0) & (ranking < capacity), weighted, F32(0)).astype(BF16)
    weights = lax.all_gather(weighted, ("group", "ingroup"), axis=0, tiled=True)

    part = jnp.dot(context, out_proj, preferred_element_type=F32).astype(BF16)
    hidden, normed = pl.pallas_call(
        spread_kernel,
        out_shape=(
            jax.ShapeDtypeStruct((rows, width), BF16),
            jax.ShapeDtypeStruct((devices, rows, width), BF16),
        ),
        in_specs=[vmem] * 3,
        out_specs=(vmem, vmem),
        scratch_shapes=[
            pltpu.VMEM((DEPTH, rows, width), BF16),
            pltpu.VMEM((DEPTH, rows, width), BF16),
            pltpu.VMEM((2, DEPTH - 1, rows, width), BF16),
            pltpu.VMEM((rows, width), F32),
            dma((CHUNKS,)), dma((CHUNKS,)),
            dma((CHUNKS, 2, DEPTH - 1)), dma((CHUNKS, 2, DEPTH - 1)),
            dma((offsets,)), dma((offsets,)),
            dma((offsets, 2)), dma((offsets, 2)),
            dma((offsets, 2)), dma((offsets, 2)),
            dma((offsets, 4)), dma((offsets, 4)),
        ],
        compiler_params=pltpu.CompilerParams(
            collective_id=0, has_side_effects=True, vmem_limit_bytes=48 * 2**20
        ),
        name="spread",
    )(part.reshape(DEPTH, SIDE, rows, width), residual, norm_gain.reshape(1, width))

    flat = normed.reshape(devices * rows, width)
    gate_part = jnp.dot(flat, gate_proj[0], preferred_element_type=F32)
    up_part = jnp.dot(flat, up_proj[0], preferred_element_type=F32)
    activated = (jax.nn.silu(gate_part) * up_part).astype(BF16)
    parts = jnp.dot(activated, down_proj[0], preferred_element_type=F32)
    expert = lax.axis_index("group") * local_experts + lax.axis_index("ingroup") // SLICES
    weight = lax.dynamic_slice_in_dim(weights, expert, 1, axis=1).astype(F32)
    parts = (parts * weight).astype(BF16)

    mixture = pl.pallas_call(
        gather_sum_kernel,
        out_shape=jax.ShapeDtypeStruct((rows, width), F32),
        in_specs=[vmem],
        out_specs=vmem,
        scratch_shapes=[
            pltpu.VMEM((DEPTH, SIDE, SIDE, rows, width), BF16),
            pltpu.VMEM((DEPTH, SIDE, SIDE, rows, width), BF16),
            pltpu.VMEM((DEPTH, rows, width // 2), BF16),
            pltpu.VMEM((DEPTH, rows, width // 2), BF16),
            pltpu.VMEM((DEPTH, rows, width), BF16),
            pltpu.VMEM((DEPTH, rows, width), BF16),
            pltpu.VMEM((DEPTH, rows, width), BF16),
            pltpu.VMEM((2, DEPTH - 1, rows, width), BF16),
            dma((offsets,)), dma((offsets,)),
            dma((offsets, 2)), dma((offsets, 2)),
            dma((offsets, 2)), dma((offsets, 2)),
            dma((2, DEPTH - 1)), dma((2, DEPTH - 1)),
        ],
        compiler_params=pltpu.CompilerParams(
            collective_id=1, has_side_effects=True, vmem_limit_bytes=48 * 2**20
        ),
        name="gather_sum",
    )(parts.reshape(SIDE, 2, DEPTH, SIDE, rows, width))
    return (hidden.astype(F32) + mixture).astype(BF16)


def solution(mesh):
    in_specs = (
        P("group", "ingroup"),
        P("ingroup", None),
        P(("group", "ingroup"), None),
        P(),
        P(("group", "ingroup"), None),
        P(("group", "ingroup"), None),
        P(("group", "ingroup"), None, None),
        P(("group", "ingroup"), None, None),
        P(("group", "ingroup"), None, None),
    )
    out_specs = P(("group", "ingroup"), None)
    sizes = (mesh.shape["group"], mesh.shape["ingroup"])
    body = local_dense if sizes == (2 * SIDE, SIDE * DEPTH) else local
    return jax.shard_map(body, mesh=mesh, in_specs=in_specs, out_specs=out_specs, check_vma=False)
```

```python
import functools

import jax
import jax.numpy as jnp
from jax import lax
from jax.experimental import pallas as pl
from jax.experimental.pallas import tpu as pltpu
from jax.sharding import PartitionSpec as P

TOPK = 8
SLICES = 4


def slice_output(arrived, gate_block, up_block, down_block):
    shape_in = arrived.shape
    flat_rows = arrived.reshape(-1, shape_in[-1])
    gate_part = jnp.dot(flat_rows, gate_block, preferred_element_type=jnp.float32)
    up_part = jnp.dot(flat_rows, up_block, preferred_element_type=jnp.float32)
    activated = (jax.nn.silu(gate_part) * up_part).astype(jnp.bfloat16)
    partial_out = jnp.dot(activated, down_block, preferred_element_type=jnp.float32).astype(
        jnp.bfloat16
    )
    return partial_out.reshape(shape_in[0], shape_in[1], down_block.shape[1])


def local(context, out_proj, residual, norm_gain, expert_ids, gates, gate_proj, up_proj, down_proj):
    group_count = lax.axis_size("group")
    member_count = lax.axis_size("ingroup")
    rows_here = residual.shape[0]
    model_width = residual.shape[1]
    local_experts = member_count // SLICES
    expert_total = group_count * local_experts
    capacity = min(rows_here, max(2, rows_here * TOPK * 5 // (4 * expert_total)))
    attended = lax.psum_scatter(
        jnp.dot(context, out_proj, preferred_element_type=jnp.float32),
        "ingroup",
        scatter_dimension=0,
        tiled=True,
    )
    hidden = (residual.astype(jnp.float32) + attended).astype(jnp.bfloat16)
    hidden_wide = hidden.astype(jnp.float32)
    inverse = lax.rsqrt(jnp.mean(hidden_wide * hidden_wide, axis=1, keepdims=True) + 1e-06)
    normed = (hidden_wide * inverse * norm_gain).astype(jnp.bfloat16)
    expert_iota = jnp.arange(expert_total, dtype=jnp.int32)
    matches = expert_ids[:, :, None] == expert_iota[None, None, :]
    picked = jnp.any(matches, axis=1)
    weighted = jnp.sum(
        jnp.where(matches, gates.astype(jnp.float32)[:, :, None], jnp.float32(0)), axis=1
    )
    gate_block = gate_proj[0]
    up_block = up_proj[0]
    down_block = down_proj[0]
    capacity_iota = jnp.arange(capacity, dtype=jnp.int32)
    picked_grid = picked.reshape(rows_here, group_count, local_experts)
    touched = jnp.any(picked_grid, axis=2).astype(jnp.int32)
    placed_at = jnp.cumsum(touched, axis=0) - touched
    slot_iota = jnp.arange(rows_here, dtype=jnp.int32)
    selector = (touched.T[:, None, :] > 0) & (placed_at.T[:, None, :] == slot_iota[None, :, None])
    selector_half = selector.astype(jnp.bfloat16)
    outgoing = jnp.einsum(
        "gst,td->gsd", selector_half, normed, preferred_element_type=jnp.float32
    ).astype(jnp.bfloat16)
    gate_grid = weighted.reshape(rows_here, group_count, local_experts).astype(jnp.bfloat16)
    outgoing_gates = jnp.einsum(
        "gst,tgl->gsl", selector_half, gate_grid, preferred_element_type=jnp.float32
    ).astype(jnp.bfloat16)
    arrived_rows, arrived_gates = (
        lax.all_to_all(outgoing, "group", split_axis=0, concat_axis=0, tiled=True),
        lax.all_to_all(outgoing_gates, "group", split_axis=0, concat_axis=0, tiled=True),
    )
    wanted = (arrived_gates > 0).astype(jnp.int32)
    relay_rank = jnp.cumsum(wanted, axis=1) - wanted
    relay_admit = (wanted > 0) & (relay_rank < capacity)
    admit_order = relay_admit.transpose(2, 0, 1)
    rank_order = relay_rank.transpose(2, 0, 1)
    placing = admit_order[:, :, None, :] & (
        rank_order[:, :, None, :] == capacity_iota[None, None, :, None]
    )
    placing_half = placing.astype(jnp.bfloat16)
    expert_rows = jnp.einsum(
        "lgcs,gsd->lgcd", placing_half, arrived_rows, preferred_element_type=jnp.float32
    ).astype(jnp.bfloat16)
    expert_rows = expert_rows.reshape(local_experts, group_count * capacity, model_width)
    dispatch = jnp.broadcast_to(
        expert_rows[:, None], (local_experts, SLICES, group_count * capacity, model_width)
    )
    dispatch = dispatch.reshape(member_count, group_count * capacity, model_width)
    returned = lax.all_to_all(
        slice_output(
            lax.all_to_all(dispatch, "ingroup", split_axis=0, concat_axis=0, tiled=True),
            gate_block,
            up_block,
            down_block,
        ),
        "ingroup",
        split_axis=0,
        concat_axis=0,
        tiled=True,
    )
    returned = returned.reshape(local_experts, SLICES, group_count, capacity, model_width)
    scaled = placing_half * arrived_gates.transpose(2, 0, 1)[:, :, None, :]
    group_out = jnp.einsum("lgcs,lugcd->gsd", scaled, returned, preferred_element_type=jnp.float32)
    back_home = lax.all_to_all(group_out, "group", split_axis=0, concat_axis=0, tiled=True)
    group_iota = jnp.arange(group_count, dtype=jnp.int32)
    fetched = back_home[group_iota[:, None], placed_at.T]
    mixture = jnp.sum(jnp.where(touched.T[:, :, None] > 0, fetched, jnp.float32(0)), axis=0)
    return (hidden_wide + mixture).astype(jnp.bfloat16)


SIDE = 2
DEPTH = 4
CHUNKS = 4
PASSES = 2
SIDE_COLUMNS = 128
OFFSETS = (0, 1, -1, 2, -2, 3, -3)
MESH = pl.DeviceIdType.MESH
BF16 = jnp.bfloat16
F32 = jnp.float32


class Place:
    def __init__(self):
        group, member = lax.axis_index("group"), lax.axis_index("ingroup")
        self.y, self.c = lax.div(group, 2), lax.rem(group, 2)
        self.z, self.x = lax.div(member, SIDE), lax.rem(member, SIDE)
        self.xo, self.yo, self.co = 1 - self.x, 1 - self.y, 1 - self.c
        self.at_x = {"group": group, "ingroup": self.z * SIDE + self.xo}
        self.at_y = {"group": self.yo * 2 + self.c, "ingroup": member}
        self.at_core = {"group": self.y * 2 + self.co, "ingroup": member}

    def at_z(self, step):
        z = lax.rem(self.z + step + DEPTH, DEPTH)
        return {"group": self.y * 2 + self.c, "ingroup": z * SIDE + self.x}

    def has_z(self, offset):
        return jnp.logical_and(self.z + offset >= 0, self.z + offset < DEPTH)

    def meet(self):
        barrier = pltpu.get_barrier_semaphore()
        for device in (self.at_x, self.at_y, self.at_core, self.at_z(1), self.at_z(-1)):
            pl.semaphore_signal(barrier, inc=1, device_id=device, device_id_type=MESH)
        pl.semaphore_wait(barrier, 5)


def remote(source, target, send, recv, device):
    return pltpu.make_async_remote_copy(
        src_ref=source, dst_ref=target, send_sem=send, recv_sem=recv, device_id=device,
        device_id_type=MESH,
    )


def chain_z(place, sums, slots, send, recv, columns, order=(3, 2, 1)):
    z = place.z
    for k in order:
        for way, step in enumerate((1, -1)):
            @pl.when(place.has_z(step * k))
            def _():
                block = sums.at[z + step * k, :, columns]
                if k < DEPTH - 1:
                    @pl.when(place.has_z(-step))
                    def _():
                        landed = slots.at[way, k, :, columns]
                        remote(landed, landed, send.at[way, k], recv.at[way, k], place.at_z(step)).wait_recv()
                        block[...] = (block[...].astype(F32) + landed[...].astype(F32)).astype(BF16)
                remote(
                    block, slots.at[way, k - 1, :, columns], send.at[way, k - 1], recv.at[way, k - 1],
                    place.at_z(step),
                ).start()


def chain_z_end(place, slots, total, send, recv, columns):
    for way, step in enumerate((1, -1)):
        @pl.when(place.has_z(-step))
        def _():
            landed = slots.at[way, 0, :, columns]
            remote(landed, landed, send.at[way, 0], recv.at[way, 0], place.at_z(step)).wait_recv()
            total[:, columns] += landed[...].astype(F32)


def chain_z_sent(place, sums, slots, send, recv, columns):
    for k in (3, 2, 1):
        for way, step in enumerate((1, -1)):
            @pl.when(place.has_z(step * k))
            def _():
                remote(
                    sums.at[place.z + step * k, :, columns], slots.at[way, k - 1, :, columns],
                    send.at[way, k - 1], recv.at[way, k - 1], place.at_z(step),
                ).wait_send()


def layer_kernel(
    context, out_proj, residual, gain, weighted, gate_proj, up_proj, down_proj, out,
    proj, gate, up, down, part, x_slots, sums, z_slots, total, hidden, rows, act, parts,
    core_slots, sums2, a_slots, b_slots, x_slots2, y_slots2, own, z_slots2,
    w_sem, proj_sem, x_send, x_recv, z_send, z_recv,
    a_send, a_recv, b_send, b_recv, d_send, d_recv, c_send, c_recv,
    core_send, core_recv, e_send, e_recv, f_send, f_recv, z2_send, z2_recv,
):
    place = Place()
    x, y, z, c, xo, yo, co = place.x, place.y, place.z, place.c, place.xo, place.yo, place.co
    rows_here, width = residual.shape
    chunk = width // CHUNKS
    span = width // PASSES
    block_rows = rows_here * SIDE * 2 * DEPTH
    cuts = [pl.ds(i * chunk, chunk) for i in range(CHUNKS)]
    extra = pl.ds(width, SIDE_COLUMNS)
    passes = [pl.ds(0, span), pl.ds(span, span + SIDE_COLUMNS)]

    def each(i, body):
        pl.when(place.has_z(-OFFSETS[i]))(body)

    def proj_copy(i):
        return pltpu.make_async_copy(out_proj.at[:, cuts[i]], proj.at[i % 2], proj_sem.at[i])

    weight_copies = [
        pltpu.make_async_copy(source.at[0], target, w_sem.at[i])
        for i, (source, target) in enumerate(((gate_proj, gate), (up_proj, up), (down_proj, down)))
    ]
    proj_copy(0).start()
    proj_copy(1).start()
    place.meet()

    def x_copy(i):
        return remote(
            part.at[:, xo, :, cuts[i]], x_slots.at[:, :, cuts[i]], x_send.at[i], x_recv.at[i], place.at_x
        )

    tile = 256
    for i in range(CHUNKS):
        proj_copy(i).wait()

        def multiply(t, carry, i=i):
            inside = pl.ds(pl.multiple_of(t * tile, tile), tile)
            columns = pl.ds(pl.multiple_of(t * tile + i * chunk, tile), tile)
            product = jnp.dot(context[...], proj[i % 2, :, inside], preferred_element_type=F32)
            part[:, :, :, columns] = product.astype(BF16).reshape(DEPTH, SIDE, rows_here, tile)
            return carry

        lax.fori_loop(0, chunk // tile, multiply, 0)
        x_copy(i).start()
        if i + 2 < CHUNKS:
            proj_copy(i + 2).start()
    for copy in weight_copies:
        copy.start()

    def head_sum(i):
        x_copy(i).wait_recv()
        for d in range(DEPTH):
            sums[d, :, cuts[i]] = (
                part[d, x, :, cuts[i]].astype(F32) + x_slots[d, :, cuts[i]].astype(F32)
            ).astype(BF16)
        total[:, cuts[i]] = residual[:, cuts[i]].astype(F32) + sums[z, :, cuts[i]].astype(F32)
        chain_z(place, sums, z_slots, z_send.at[i], z_recv.at[i], cuts[i])

    def index(y, c, z, x):
        return ((y * 2 + c) * DEPTH + z) * SIDE + x

    mine = index(y, c, z, x)
    squares = []

    def settle(q):
        per = CHUNKS // PASSES
        for i in range(q * per, (q + 1) * per):
            chain_z_end(place, z_slots, total, z_send.at[i], z_recv.at[i], cuts[i])
        columns = pl.ds(q * span, span)
        rounded = total[:, columns].astype(BF16)
        hidden[:, columns] = rounded
        wide = rounded.astype(F32)
        squares.append(jnp.sum(wide * wide, axis=1, keepdims=True))
        rows[mine, :, columns] = (wide * gain[:, columns]).astype(BF16)
        if q == PASSES - 1:
            inverse = lax.rsqrt(sum(squares) / width + 1e-06)
            high = inverse.astype(BF16).astype(F32)
            lane = lax.broadcasted_iota(jnp.int32, (rows_here, SIDE_COLUMNS), 1)
            side = jnp.where(
                lane == SIDE_COLUMNS - 2, high,
                jnp.where(lane == SIDE_COLUMNS - 1, inverse - high, weighted[...].astype(F32)),
            )
            rows[mine, :, extra] = side.astype(BF16)

    def here(i, by_x, by_y):
        return index(yo if by_y else y, c, z - OFFSETS[i], xo if by_x else x)

    def copy_to(device, block, q, send, recv):
        ref = rows.at[block, :, passes[q]]
        return remote(ref, ref, send, recv, device)

    def z_copy(q, i, step):
        there = OFFSETS.index(OFFSETS[i] + step)
        return copy_to(place.at_z(step), here(i, 0, 0), q, a_send.at[q, there], a_recv.at[q, there])

    def z_steps(i):
        offset = OFFSETS[i]
        return [s for s in (1, -1) if offset * s >= 0 and abs(offset + s) < DEPTH]

    def x_full(q, i, by_x=0):
        return copy_to(place.at_x, here(i, by_x, 0), q, b_send.at[q, i, 0], b_recv.at[q, i, 0])

    def y_full(q, i, by_y=0):
        return copy_to(place.at_y, here(i, 0, by_y), q, b_send.at[q, i, 1], b_recv.at[q, i, 1])

    def y_on(q, i, by_y=0):
        return copy_to(place.at_y, here(i, 1, by_y), q, d_send.at[q, i], d_recv.at[q, i])

    def core_copy(q, i, by_x, by_y):
        k = by_x * 2 + by_y
        return copy_to(place.at_core, here(i, by_x, by_y), q, c_send.at[q, i, k], c_recv.at[q, i, k])

    def core_wait(q, i, by_x, by_y):
        k = by_x * 2 + by_y
        block = index(yo if by_y else y, co, z - OFFSETS[i], xo if by_x else x)
        copy_to(place.at_core, block, q, c_send.at[q, i, k], c_recv.at[q, i, k]).wait_recv()

    def along_z(q, i):
        def body():
            if i > 0:
                copy_to(place.at_x, here(i, 0, 0), q, a_send.at[q, i], a_recv.at[q, i]).wait_recv()
            for step in z_steps(i):
                @pl.when(place.has_z(step))
                def _():
                    z_copy(q, i, step).start()
            x_full(q, i).start()
            y_full(q, i).start()
            core_copy(q, i, 0, 0).start()

        each(i, body)

    def along_xy(q, i):
        def body():
            x_full(q, i, 1).wait_recv()
            y_on(q, i).start()
            core_copy(q, i, 1, 0).start()
            y_full(q, i, 1).wait_recv()
            core_copy(q, i, 0, 1).start()

        each(i, body)

    def along_diagonal(q, i):
        def body():
            y_on(q, i, 1).wait_recv()
            core_copy(q, i, 1, 1).start()

        each(i, body)

    near = ((0,), (1, 2), (3, 4), (5, 6))

    def level(action, q, t):
        if 0 <= t < DEPTH:
            for i in near[t]:
                action(q, i)

    head_sum(0)
    head_sum(1)
    settle(0)
    level(along_z, 0, 0)
    head_sum(2)
    level(along_z, 0, 1)
    head_sum(3)
    level(along_xy, 0, 0)
    settle(1)
    for t in range(DEPTH + 1):
        level(along_z, 1, t)
        level(along_z, 0, t + 2)
        level(along_xy, 0, t + 1)
        level(along_xy, 1, t - 1)
        level(along_diagonal, 0, t)
        level(along_diagonal, 1, t - 2)

    def all_blocks(action):
        for q in range(PASSES):
            for i in range(len(OFFSETS)):
                each(i, lambda q=q, i=i: action(q, i))

    def cores_near(q, i):
        core_wait(q, i, 0, 0)
        core_wait(q, i, 1, 0)

    def cores_far(q, i):
        core_wait(q, i, 0, 1)
        core_wait(q, i, 1, 1)

    member_count = SIDE * DEPTH
    expert = (y * 2 + c) * (member_count // SLICES) + lax.div(z * SIDE + x, SLICES)
    half_blocks = 2 * DEPTH * SIDE

    def side_of(j):
        side = rows[pl.ds(j * half_blocks, half_blocks), :, extra].reshape(block_rows, SIDE_COLUMNS)
        return side.astype(F32), lax.broadcasted_iota(jnp.int32, (block_rows, SIDE_COLUMNS), 1)

    def widen(j):
        depth = 1024

        def multiply(t, carry):
            columns = pl.ds(pl.multiple_of(t * depth, depth), depth)
            block = rows[pl.ds(j * half_blocks, half_blocks), :, columns].reshape(block_rows, depth)
            return (
                carry[0] + jnp.dot(block, gate[columns, :], preferred_element_type=F32),
                carry[1] + jnp.dot(block, up[columns, :], preferred_element_type=F32),
            )

        zeros = jnp.zeros((block_rows, gate.shape[1]), F32)
        gate_part, up_part = lax.fori_loop(0, width // depth, multiply, (zeros, zeros))
        side, lane = side_of(j)
        inverse = jnp.sum(jnp.where(lane >= SIDE_COLUMNS - 2, side, 0.0), axis=1, keepdims=True)
        gate_part = gate_part * inverse
        act[j] = (gate_part / (1.0 + jnp.exp(-gate_part)) * (up_part * inverse)).astype(BF16)

    def narrow(j):
        side, lane = side_of(j)
        weight = jnp.sum(jnp.where(lane == expert, side, 0.0), axis=1, keepdims=True)
        step = 512

        def multiply(t, carry):
            columns = pl.ds(pl.multiple_of(t * step, step), step)
            product = jnp.dot(act[j], down[:, columns], preferred_element_type=F32) * weight
            parts[j, :, :, :, :, columns] = product.astype(BF16).reshape(
                2, DEPTH, SIDE, rows_here, step
            )
            return carry

        lax.fori_loop(0, width // step, multiply, 0)

    for copy in weight_copies:
        copy.wait()
    all_blocks(cores_near)
    widen(y)
    level(along_diagonal, 1, DEPTH - 1)
    all_blocks(cores_far)
    widen(yo)

    half = width // 2
    cut_a, cut_b, whole = pl.ds(0, half), pl.ds(half, half), pl.ds(0, width)
    far = (6, 5, 4, 3, 2, 1, 0)

    def part_copy(i, k):
        d = z - OFFSETS[i]
        j = (yo, y)[k]
        return remote(
            parts.at[j, co, d], core_slots.at[d, j], core_send.at[i, k], core_recv.at[i, k], place.at_core
        )

    def diagonal_a(i):
        d = z - OFFSETS[i]
        return remote(
            sums2.at[d, yo, xo, :, cut_a], a_slots.at[d], e_send.at[i, 0], e_recv.at[i, 0], place.at_y
        )

    def diagonal_b(i):
        d = z - OFFSETS[i]
        return remote(
            sums2.at[d, yo, xo, :, cut_b], b_slots.at[d], e_send.at[i, 1], e_recv.at[i, 1], place.at_x
        )

    def full_x(i):
        d = z - OFFSETS[i]
        return remote(sums2.at[d, y, xo], x_slots2.at[d], f_send.at[i, 0], f_recv.at[i, 0], place.at_x)

    def full_y(i):
        d = z - OFFSETS[i]
        return remote(sums2.at[d, yo, x], y_slots2.at[d], f_send.at[i, 1], f_recv.at[i, 1], place.at_y)

    def first(i):
        def body():
            d = z - OFFSETS[i]
            for k, j in enumerate((yo, y)):
                part_copy(i, k).wait_recv()
                for m in (xo, x):
                    sums2[d, j, m] = (
                        parts[j, c, d, m].astype(F32) + core_slots[d, j, m].astype(F32)
                    ).astype(BF16)
                    if k == 0 and m is xo:
                        diagonal_a(i).start()
                        diagonal_b(i).start()

        each(i, body)

    def second(i):
        def body():
            d = z - OFFSETS[i]
            diagonal_a(i).wait_recv()
            sums2[d, y, xo, :, cut_a] = (
                sums2[d, y, xo, :, cut_a].astype(F32) + a_slots[d].astype(F32)
            ).astype(BF16)
            full_x(i).start()
            diagonal_b(i).wait_recv()
            sums2[d, yo, x, :, cut_b] = (
                sums2[d, yo, x, :, cut_b].astype(F32) + b_slots[d].astype(F32)
            ).astype(BF16)
            full_y(i).start()

        each(i, body)

    def third(i):
        def body():
            d = z - OFFSETS[i]
            full_x(i).wait_recv()
            full_y(i).wait_recv()
            own[d] = (
                sums2[d, y, x].astype(F32) + x_slots2[d].astype(F32) + y_slots2[d].astype(F32)
            ).astype(BF16)

        each(i, body)

    narrow(yo)
    for i in far:
        each(i, lambda i=i: part_copy(i, 0).start())
    narrow(y)
    for i in far:
        each(i, lambda i=i: part_copy(i, 1).start())
    levels = ((6, 5), (4, 3), (2, 1), (0,))
    for t in range(len(levels) + 2):
        for i in levels[t] if t < len(levels) else ():
            first(i)
        for i in levels[t - 1] if 0 <= t - 1 < len(levels) else ():
            second(i)
        if 0 <= t - 2 < len(levels):
            for i in levels[t - 2]:
                third(i)
            if t - 2 < DEPTH - 1:
                chain_z(place, own, z_slots2, z2_send, z2_recv, whole, order=(DEPTH - 1 - (t - 2),))
    out[...] = hidden[...].astype(F32) + own[z].astype(F32)
    chain_z_end(place, z_slots2, out, z2_send, z2_recv, whole)

    for i in range(CHUNKS):
        x_copy(i).wait_send()
        chain_z_sent(place, sums, z_slots, z_send.at[i], z_recv.at[i], cuts[i])

    def sent(q, i):
        for step in z_steps(i):
            @pl.when(place.has_z(step))
            def _():
                z_copy(q, i, step).wait_send()
        for copy in (x_full(q, i), y_full(q, i), y_on(q, i)):
            copy.wait_send()
        for k in range(4):
            core_copy(q, i, k // 2, k % 2).wait_send()

    all_blocks(sent)
    for i in far:
        def body(i=i):
            for copy in (
                part_copy(i, 0), part_copy(i, 1), diagonal_a(i), diagonal_b(i), full_x(i), full_y(i)
            ):
                copy.wait_send()

        each(i, body)
    chain_z_sent(place, own, z_slots2, z2_send, z2_recv, whole)


def local_dense(
    context, out_proj, residual, norm_gain, expert_ids, gates, gate_proj, up_proj, down_proj
):
    group_count = lax.axis_size("group")
    member_count = lax.axis_size("ingroup")
    devices = group_count * member_count
    rows, width = residual.shape
    inner = gate_proj.shape[2]
    expert_total = group_count * (member_count // SLICES)
    capacity = min(rows, max(2, rows * TOPK * 5 // (4 * expert_total)))
    offsets = len(OFFSETS)
    dma = pltpu.SemaphoreType.DMA
    vmem = pl.BlockSpec(memory_space=pltpu.VMEM)
    anywhere = pl.BlockSpec(memory_space=pl.ANY)

    expert_iota = jnp.arange(SIDE_COLUMNS, dtype=jnp.int32)
    matches = expert_ids[:, :, None] == expert_iota[None, None, :]
    picked = jnp.any(matches, axis=1).astype(F32)
    before = jnp.tril(jnp.ones((rows, rows), F32), -1)
    ranking = jnp.dot(before, picked)
    weighted = jnp.sum(jnp.where(matches, gates.astype(F32)[:, :, None], F32(0)), axis=1)
    weighted = jnp.where((picked > 0) & (ranking < capacity), weighted, F32(0)).astype(BF16)

    def half(*shape):
        return pltpu.VMEM(shape, BF16)

    summed = pl.pallas_call(
        layer_kernel,
        out_shape=jax.ShapeDtypeStruct((rows, width), F32),
        in_specs=[vmem, anywhere, vmem, vmem, vmem, anywhere, anywhere, anywhere],
        out_specs=vmem,
        scratch_shapes=[
            half(2, context.shape[1], width // CHUNKS),
            half(width, inner), half(width, inner), half(inner, width),
            half(DEPTH, SIDE, rows, width),
            half(DEPTH, rows, width),
            half(DEPTH, rows, width),
            half(2, DEPTH - 1, rows, width),
            pltpu.VMEM((rows, width), F32),
            half(rows, width),
            half(devices, rows, width + SIDE_COLUMNS),
            half(SIDE, devices * rows // SIDE, inner),
            half(SIDE, 2, DEPTH, SIDE, rows, width),
            half(DEPTH, SIDE, SIDE, rows, width),
            half(DEPTH, SIDE, SIDE, rows, width),
            half(DEPTH, rows, width // 2),
            half(DEPTH, rows, width // 2),
            half(DEPTH, rows, width),
            half(DEPTH, rows, width),
            half(DEPTH, rows, width),
            half(2, DEPTH - 1, rows, width),
            dma((3,)), dma((CHUNKS,)),
            dma((CHUNKS,)), dma((CHUNKS,)),
            dma((CHUNKS, 2, DEPTH - 1)), dma((CHUNKS, 2, DEPTH - 1)),
            dma((PASSES, offsets)), dma((PASSES, offsets)),
            dma((PASSES, offsets, 2)), dma((PASSES, offsets, 2)),
            dma((PASSES, offsets)), dma((PASSES, offsets)),
            dma((PASSES, offsets, 4)), dma((PASSES, offsets, 4)),
            dma((offsets, 2)), dma((offsets, 2)),
            dma((offsets, 2)), dma((offsets, 2)),
            dma((offsets, 2)), dma((offsets, 2)),
            dma((2, DEPTH - 1)), dma((2, DEPTH - 1)),
        ],
        compiler_params=pltpu.CompilerParams(
            collective_id=0, has_side_effects=True, vmem_limit_bytes=58 * 2**20
        ),
        name="layer",
    )(
        context, out_proj, residual, norm_gain.reshape(1, width), weighted, gate_proj, up_proj,
        down_proj,
    )
    return summed.astype(BF16)


def solution(mesh):
    in_specs = (
        P("group", "ingroup"),
        P("ingroup", None),
        P(("group", "ingroup"), None),
        P(),
        P(("group", "ingroup"), None),
        P(("group", "ingroup"), None),
        P(("group", "ingroup"), None, None),
        P(("group", "ingroup"), None, None),
        P(("group", "ingroup"), None, None),
    )
    out_specs = P(("group", "ingroup"), None)
    sizes = (mesh.shape["group"], mesh.shape["ingroup"])
    body = local_dense if sizes == (2 * SIDE, SIDE * DEPTH) else local
    return jax.shard_map(body, mesh=mesh, in_specs=in_specs, out_specs=out_specs, check_vma=False)
```

```python
import functools

import jax
import jax.numpy as jnp
from jax import lax
from jax.experimental import pallas as pl
from jax.experimental.pallas import tpu as pltpu
from jax.sharding import PartitionSpec as P

TOPK = 8
SLICES = 4


def slice_output(arrived, gate_block, up_block, down_block):
    shape_in = arrived.shape
    flat_rows = arrived.reshape(-1, shape_in[-1])
    gate_part = jnp.dot(flat_rows, gate_block, preferred_element_type=jnp.float32)
    up_part = jnp.dot(flat_rows, up_block, preferred_element_type=jnp.float32)
    activated = (jax.nn.silu(gate_part) * up_part).astype(jnp.bfloat16)
    partial_out = jnp.dot(activated, down_block, preferred_element_type=jnp.float32).astype(
        jnp.bfloat16
    )
    return partial_out.reshape(shape_in[0], shape_in[1], down_block.shape[1])


def local(context, out_proj, residual, norm_gain, expert_ids, gates, gate_proj, up_proj, down_proj):
    group_count = lax.axis_size("group")
    member_count = lax.axis_size("ingroup")
    rows_here = residual.shape[0]
    model_width = residual.shape[1]
    local_experts = member_count // SLICES
    expert_total = group_count * local_experts
    capacity = min(rows_here, max(2, rows_here * TOPK * 5 // (4 * expert_total)))
    attended = lax.psum_scatter(
        jnp.dot(context, out_proj, preferred_element_type=jnp.float32),
        "ingroup",
        scatter_dimension=0,
        tiled=True,
    )
    hidden = (residual.astype(jnp.float32) + attended).astype(jnp.bfloat16)
    hidden_wide = hidden.astype(jnp.float32)
    inverse = lax.rsqrt(jnp.mean(hidden_wide * hidden_wide, axis=1, keepdims=True) + 1e-06)
    normed = (hidden_wide * inverse * norm_gain).astype(jnp.bfloat16)
    expert_iota = jnp.arange(expert_total, dtype=jnp.int32)
    matches = expert_ids[:, :, None] == expert_iota[None, None, :]
    picked = jnp.any(matches, axis=1)
    weighted = jnp.sum(
        jnp.where(matches, gates.astype(jnp.float32)[:, :, None], jnp.float32(0)), axis=1
    )
    gate_block = gate_proj[0]
    up_block = up_proj[0]
    down_block = down_proj[0]
    capacity_iota = jnp.arange(capacity, dtype=jnp.int32)
    picked_grid = picked.reshape(rows_here, group_count, local_experts)
    touched = jnp.any(picked_grid, axis=2).astype(jnp.int32)
    placed_at = jnp.cumsum(touched, axis=0) - touched
    slot_iota = jnp.arange(rows_here, dtype=jnp.int32)
    selector = (touched.T[:, None, :] > 0) & (placed_at.T[:, None, :] == slot_iota[None, :, None])
    selector_half = selector.astype(jnp.bfloat16)
    outgoing = jnp.einsum(
        "gst,td->gsd", selector_half, normed, preferred_element_type=jnp.float32
    ).astype(jnp.bfloat16)
    gate_grid = weighted.reshape(rows_here, group_count, local_experts).astype(jnp.bfloat16)
    outgoing_gates = jnp.einsum(
        "gst,tgl->gsl", selector_half, gate_grid, preferred_element_type=jnp.float32
    ).astype(jnp.bfloat16)
    arrived_rows, arrived_gates = (
        lax.all_to_all(outgoing, "group", split_axis=0, concat_axis=0, tiled=True),
        lax.all_to_all(outgoing_gates, "group", split_axis=0, concat_axis=0, tiled=True),
    )
    wanted = (arrived_gates > 0).astype(jnp.int32)
    relay_rank = jnp.cumsum(wanted, axis=1) - wanted
    relay_admit = (wanted > 0) & (relay_rank < capacity)
    admit_order = relay_admit.transpose(2, 0, 1)
    rank_order = relay_rank.transpose(2, 0, 1)
    placing = admit_order[:, :, None, :] & (
        rank_order[:, :, None, :] == capacity_iota[None, None, :, None]
    )
    placing_half = placing.astype(jnp.bfloat16)
    expert_rows = jnp.einsum(
        "lgcs,gsd->lgcd", placing_half, arrived_rows, preferred_element_type=jnp.float32
    ).astype(jnp.bfloat16)
    expert_rows = expert_rows.reshape(local_experts, group_count * capacity, model_width)
    dispatch = jnp.broadcast_to(
        expert_rows[:, None], (local_experts, SLICES, group_count * capacity, model_width)
    )
    dispatch = dispatch.reshape(member_count, group_count * capacity, model_width)
    returned = lax.all_to_all(
        slice_output(
            lax.all_to_all(dispatch, "ingroup", split_axis=0, concat_axis=0, tiled=True),
            gate_block,
            up_block,
            down_block,
        ),
        "ingroup",
        split_axis=0,
        concat_axis=0,
        tiled=True,
    )
    returned = returned.reshape(local_experts, SLICES, group_count, capacity, model_width)
    scaled = placing_half * arrived_gates.transpose(2, 0, 1)[:, :, None, :]
    group_out = jnp.einsum("lgcs,lugcd->gsd", scaled, returned, preferred_element_type=jnp.float32)
    back_home = lax.all_to_all(group_out, "group", split_axis=0, concat_axis=0, tiled=True)
    group_iota = jnp.arange(group_count, dtype=jnp.int32)
    fetched = back_home[group_iota[:, None], placed_at.T]
    mixture = jnp.sum(jnp.where(touched.T[:, :, None] > 0, fetched, jnp.float32(0)), axis=0)
    return (hidden_wide + mixture).astype(jnp.bfloat16)


SIDE = 2
DEPTH = 4
CHUNKS = 4
PASSES = 2
SIDE_COLUMNS = 128
OFFSETS = (0, 1, -1, 2, -2, 3, -3)
MESH = pl.DeviceIdType.MESH
BF16 = jnp.bfloat16
F32 = jnp.float32


class Place:
    def __init__(self):
        group, member = lax.axis_index("group"), lax.axis_index("ingroup")
        self.y, self.c = lax.div(group, 2), lax.rem(group, 2)
        self.z, self.x = lax.div(member, SIDE), lax.rem(member, SIDE)
        self.xo, self.yo, self.co = 1 - self.x, 1 - self.y, 1 - self.c
        self.at_x = {"group": group, "ingroup": self.z * SIDE + self.xo}
        self.at_y = {"group": self.yo * 2 + self.c, "ingroup": member}
        self.at_core = {"group": self.y * 2 + self.co, "ingroup": member}

    def at_z(self, step):
        z = lax.rem(self.z + step + DEPTH, DEPTH)
        return {"group": self.y * 2 + self.c, "ingroup": z * SIDE + self.x}

    def has_z(self, offset):
        return jnp.logical_and(self.z + offset >= 0, self.z + offset < DEPTH)

    def greet(self):
        barrier = pltpu.get_barrier_semaphore()
        for device in (self.at_x, self.at_y, self.at_core, self.at_z(1), self.at_z(-1)):
            pl.semaphore_signal(barrier, inc=1, device_id=device, device_id_type=MESH)

    def meet(self):
        pl.semaphore_wait(pltpu.get_barrier_semaphore(), 5)


def remote(source, target, send, recv, device):
    return pltpu.make_async_remote_copy(
        src_ref=source, dst_ref=target, send_sem=send, recv_sem=recv, device_id=device,
        device_id_type=MESH,
    )


def chain_z(place, sums, slots, send, recv, columns, order=(3, 2, 1)):
    z = place.z
    for k in order:
        for way, step in enumerate((1, -1)):
            @pl.when(place.has_z(step * k))
            def _():
                block = sums.at[z + step * k, :, columns]
                if k < DEPTH - 1:
                    @pl.when(place.has_z(-step))
                    def _():
                        landed = slots.at[way, k, :, columns]
                        remote(landed, landed, send.at[way, k], recv.at[way, k], place.at_z(step)).wait_recv()
                        block[...] = (block[...].astype(F32) + landed[...].astype(F32)).astype(BF16)
                remote(
                    block, slots.at[way, k - 1, :, columns], send.at[way, k - 1], recv.at[way, k - 1],
                    place.at_z(step),
                ).start()


def chain_z_end(place, slots, total, send, recv, columns):
    for way, step in enumerate((1, -1)):
        @pl.when(place.has_z(-step))
        def _():
            landed = slots.at[way, 0, :, columns]
            remote(landed, landed, send.at[way, 0], recv.at[way, 0], place.at_z(step)).wait_recv()
            total[:, columns] += landed[...].astype(F32)


def chain_z_sent(place, sums, slots, send, recv, columns):
    for k in (3, 2, 1):
        for way, step in enumerate((1, -1)):
            @pl.when(place.has_z(step * k))
            def _():
                remote(
                    sums.at[place.z + step * k, :, columns], slots.at[way, k - 1, :, columns],
                    send.at[way, k - 1], recv.at[way, k - 1], place.at_z(step),
                ).wait_send()


def layer_kernel(
    capacity, context, out_proj, residual, gain, ids, gates, gate_proj, up_proj, down_proj, out,
    proj, gate, up, down, part, x_slots, sums, z_slots, total, hidden, rows, act, parts,
    core_slots, sums2, a_slots, b_slots, x_slots2, y_slots2, own, z_slots2,
    w_sem, proj_sem, x_send, x_recv, z_send, z_recv,
    a_send, a_recv, b_send, b_recv, d_send, d_recv, c_send, c_recv,
    core_send, core_recv, e_send, e_recv, f_send, f_recv, z2_send, z2_recv,
):
    place = Place()
    x, y, z, c, xo, yo, co = place.x, place.y, place.z, place.c, place.xo, place.yo, place.co
    rows_here, width = residual.shape
    chunk = width // CHUNKS
    span = width // PASSES
    block_rows = rows_here * SIDE * 2 * DEPTH
    cuts = [pl.ds(i * chunk, chunk) for i in range(CHUNKS)]
    extra = pl.ds(width, SIDE_COLUMNS)
    passes = [pl.ds(0, span), pl.ds(span, span + SIDE_COLUMNS)]

    def each(i, body):
        pl.when(place.has_z(-OFFSETS[i]))(body)

    def proj_copy(i):
        return pltpu.make_async_copy(out_proj.at[:, cuts[i]], proj.at[i % 2], proj_sem.at[i])

    weight_copies = [
        pltpu.make_async_copy(source.at[0], target, w_sem.at[i])
        for i, (source, target) in enumerate(((gate_proj, gate), (up_proj, up), (down_proj, down)))
    ]
    proj_copy(0).start()
    proj_copy(1).start()
    place.greet()

    def x_copy(i):
        return remote(
            part.at[:, xo, :, cuts[i]], x_slots.at[:, :, cuts[i]], x_send.at[i], x_recv.at[i], place.at_x
        )

    tile = 256
    for i in range(CHUNKS):
        proj_copy(i).wait()

        def multiply(t, carry, i=i):
            inside = pl.ds(pl.multiple_of(t * tile, tile), tile)
            columns = pl.ds(pl.multiple_of(t * tile + i * chunk, tile), tile)
            product = jnp.dot(context[...], proj[i % 2, :, inside], preferred_element_type=F32)
            part[:, :, :, columns] = product.astype(BF16).reshape(DEPTH, SIDE, rows_here, tile)
            return carry

        lax.fori_loop(0, chunk // tile, multiply, 0)
        if i == 0:
            place.meet()
        x_copy(i).start()
        if i + 2 < CHUNKS:
            proj_copy(i + 2).start()
    for copy in weight_copies:
        copy.start()

    lane = lax.broadcasted_iota(jnp.int32, (rows_here, SIDE_COLUMNS), 1)
    down_iota = lax.broadcasted_iota(jnp.int32, (rows_here, rows_here), 0)
    across_iota = lax.broadcasted_iota(jnp.int32, (rows_here, rows_here), 1)

    def upright(line):
        spread = jnp.broadcast_to(line, (rows_here, rows_here))
        return jnp.sum(jnp.where(down_iota == across_iota, spread, 0.0), axis=1, keepdims=True)

    weighted = jnp.zeros((rows_here, SIDE_COLUMNS), F32)
    picked = jnp.zeros((rows_here, SIDE_COLUMNS), F32)
    ids_wide, gates_wide = ids[...].astype(F32), gates[...].astype(F32)
    for j in range(TOPK):
        match = lane.astype(F32) == upright(ids_wide[j : j + 1, :])
        weighted += jnp.where(match, upright(gates_wide[j : j + 1, :]), 0.0)
        picked = jnp.where(match, 1.0, picked)
    before = jnp.where(down_iota > across_iota, 1.0, 0.0).astype(BF16)
    ranking = jnp.dot(before, picked.astype(BF16), preferred_element_type=F32)
    admitted = jnp.where(ranking < capacity, picked, 0.0)
    weighted = jnp.where(admitted > 0.0, weighted, 0.0)

    def head_sum(i):
        x_copy(i).wait_recv()
        for d in range(DEPTH):
            sums[d, :, cuts[i]] = (
                part[d, x, :, cuts[i]].astype(F32) + x_slots[d, :, cuts[i]].astype(F32)
            ).astype(BF16)
        total[:, cuts[i]] = residual[:, cuts[i]].astype(F32) + sums[z, :, cuts[i]].astype(F32)
        chain(i, 3)

    def chain(i, k):
        chain_z(place, sums, z_slots, z_send.at[i], z_recv.at[i], cuts[i], order=(k,))

    def index(y, c, z, x):
        return ((y * 2 + c) * DEPTH + z) * SIDE + x

    mine = index(y, c, z, x)
    squares = []

    def settle(q):
        per = CHUNKS // PASSES
        for i in range(q * per, (q + 1) * per):
            chain_z_end(place, z_slots, total, z_send.at[i], z_recv.at[i], cuts[i])
        columns = pl.ds(q * span, span)
        rounded = total[:, columns].astype(BF16)
        hidden[:, columns] = rounded
        wide = rounded.astype(F32)
        squares.append(jnp.sum(wide * wide, axis=1, keepdims=True))
        rows[mine, :, columns] = (wide * gain[:, columns]).astype(BF16)
        if q == PASSES - 1:
            inverse = lax.rsqrt(sum(squares) / width + 1e-06)
            high = inverse.astype(BF16).astype(F32)
            side = jnp.where(
                lane == SIDE_COLUMNS - 2, high,
                jnp.where(lane == SIDE_COLUMNS - 1, inverse - high, weighted),
            )
            rows[mine, :, extra] = side.astype(BF16)

    def here(i, by_x, by_y):
        return index(yo if by_y else y, c, z - OFFSETS[i], xo if by_x else x)

    def copy_to(device, block, q, send, recv):
        ref = rows.at[block, :, passes[q]]
        return remote(ref, ref, send, recv, device)

    def z_copy(q, i, step):
        there = OFFSETS.index(OFFSETS[i] + step)
        return copy_to(place.at_z(step), here(i, 0, 0), q, a_send.at[q, there], a_recv.at[q, there])

    def z_steps(i):
        offset = OFFSETS[i]
        return [s for s in (1, -1) if offset * s >= 0 and abs(offset + s) < DEPTH]

    def x_full(q, i, by_x=0):
        return copy_to(place.at_x, here(i, by_x, 0), q, b_send.at[q, i, 0], b_recv.at[q, i, 0])

    def y_full(q, i, by_y=0):
        return copy_to(place.at_y, here(i, 0, by_y), q, b_send.at[q, i, 1], b_recv.at[q, i, 1])

    def onward(q, i, landed=0):
        device = (place.at_y, place.at_x)[q]
        block = here(i, 1, 1) if landed else here(i, 1 - q, q)
        return copy_to(device, block, q, d_send.at[q, i], d_recv.at[q, i])

    def core_copy(q, i, by_x, by_y):
        k = by_x * 2 + by_y
        return copy_to(place.at_core, here(i, by_x, by_y), q, c_send.at[q, i, k], c_recv.at[q, i, k])

    def core_wait(q, i, by_x, by_y):
        k = by_x * 2 + by_y
        block = index(yo if by_y else y, co, z - OFFSETS[i], xo if by_x else x)
        copy_to(place.at_core, block, q, c_send.at[q, i, k], c_recv.at[q, i, k]).wait_recv()

    def along_z(q, i):
        def body():
            if i > 0:
                copy_to(place.at_x, here(i, 0, 0), q, a_send.at[q, i], a_recv.at[q, i]).wait_recv()
            for step in z_steps(i):
                @pl.when(place.has_z(step))
                def _():
                    z_copy(q, i, step).start()
            x_full(q, i).start()
            y_full(q, i).start()
            core_copy(q, i, 0, 0).start()

        each(i, body)

    def along_xy(q, i):
        def body():
            arrivals = [(x_full(q, i, 1), (1, 0)), (y_full(q, i, 1), (0, 1))]
            for n in (q, 1 - q):
                arrivals[n][0].wait_recv()
                if n == q:
                    onward(q, i).start()
                core_copy(q, i, *arrivals[n][1]).start()

        each(i, body)

    def along_diagonal(q, i):
        def body():
            onward(q, i, 1).wait_recv()
            core_copy(q, i, 1, 1).start()

        each(i, body)

    near = ((0,), (1, 2), (3, 4), (5, 6))

    def level(action, q, t):
        if 0 <= t < DEPTH:
            for i in near[t]:
                action(q, i)

    head_sum(0)
    chain(0, 2)
    head_sum(1)
    chain(0, 1)
    chain(1, 2)
    head_sum(2)
    chain(1, 1)
    chain(2, 2)
    settle(0)
    level(along_z, 0, 0)
    head_sum(3)
    chain(2, 1)
    chain(3, 2)
    level(along_z, 0, 1)
    level(along_xy, 0, 0)
    chain(3, 1)
    settle(1)
    for t in range(DEPTH + 1):
        level(along_z, 1, t)
        level(along_z, 0, t + 2)
        level(along_xy, 0, t + 1)
        level(along_xy, 1, t - 1)
        level(along_diagonal, 0, t)
        level(along_diagonal, 1, t - 2)

    def all_blocks(action):
        for q in range(PASSES):
            for i in range(len(OFFSETS)):
                each(i, lambda q=q, i=i: action(q, i))

    def cores_near(q, i):
        core_wait(q, i, 0, 0)
        core_wait(q, i, 1, 0)

    def cores_far(q, i):
        core_wait(q, i, 0, 1)
        core_wait(q, i, 1, 1)

    member_count = SIDE * DEPTH
    expert = (y * 2 + c) * (member_count // SLICES) + lax.div(z * SIDE + x, SLICES)
    half_blocks = 2 * DEPTH * SIDE

    def side_of(j):
        side = rows[pl.ds(j * half_blocks, half_blocks), :, extra].reshape(block_rows, SIDE_COLUMNS)
        return side.astype(F32), lax.broadcasted_iota(jnp.int32, (block_rows, SIDE_COLUMNS), 1)

    def widen(j):
        depth = 1024

        def multiply(t, carry):
            columns = pl.ds(pl.multiple_of(t * depth, depth), depth)
            block = rows[pl.ds(j * half_blocks, half_blocks), :, columns].reshape(block_rows, depth)
            return (
                carry[0] + jnp.dot(block, gate[columns, :], preferred_element_type=F32),
                carry[1] + jnp.dot(block, up[columns, :], preferred_element_type=F32),
            )

        zeros = jnp.zeros((block_rows, gate.shape[1]), F32)
        gate_part, up_part = lax.fori_loop(0, width // depth, multiply, (zeros, zeros))
        side, lane = side_of(j)
        inverse = jnp.sum(jnp.where(lane >= SIDE_COLUMNS - 2, side, 0.0), axis=1, keepdims=True)
        gate_part = gate_part * inverse
        act[j] = (gate_part / (1.0 + jnp.exp(-gate_part)) * (up_part * inverse)).astype(BF16)

    def narrow(j):
        side, lane = side_of(j)
        weight = jnp.sum(jnp.where(lane == expert, side, 0.0), axis=1, keepdims=True)
        step = 512

        def multiply(t, carry):
            columns = pl.ds(pl.multiple_of(t * step, step), step)
            product = jnp.dot(act[j], down[:, columns], preferred_element_type=F32) * weight
            parts[j, :, :, :, :, columns] = product.astype(BF16).reshape(
                2, DEPTH, SIDE, rows_here, step
            )
            return carry

        lax.fori_loop(0, width // step, multiply, 0)

    for copy in weight_copies:
        copy.wait()
    all_blocks(cores_near)
    widen(y)
    level(along_diagonal, 1, DEPTH - 1)
    all_blocks(cores_far)
    widen(yo)

    half = width // 2
    cut_a, cut_b, whole = pl.ds(0, half), pl.ds(half, half), pl.ds(0, width)
    far = (6, 5, 4, 3, 2, 1, 0)

    def part_copy(i, k):
        d = z - OFFSETS[i]
        j = (yo, y)[k]
        return remote(
            parts.at[j, co, d], core_slots.at[d, j], core_send.at[i, k], core_recv.at[i, k], place.at_core
        )

    def diagonal_a(i):
        d = z - OFFSETS[i]
        return remote(
            sums2.at[d, yo, xo, :, cut_a], a_slots.at[d], e_send.at[i, 0], e_recv.at[i, 0], place.at_y
        )

    def diagonal_b(i):
        d = z - OFFSETS[i]
        return remote(
            sums2.at[d, yo, xo, :, cut_b], b_slots.at[d], e_send.at[i, 1], e_recv.at[i, 1], place.at_x
        )

    def full_x(i):
        d = z - OFFSETS[i]
        return remote(sums2.at[d, y, xo], x_slots2.at[d], f_send.at[i, 0], f_recv.at[i, 0], place.at_x)

    def full_y(i):
        d = z - OFFSETS[i]
        return remote(sums2.at[d, yo, x], y_slots2.at[d], f_send.at[i, 1], f_recv.at[i, 1], place.at_y)

    def first(i, k):
        def body():
            d = z - OFFSETS[i]
            j = (yo, y)[k]
            part_copy(i, k).wait_recv()
            for m in (xo, x):
                sums2[d, j, m] = (
                    parts[j, c, d, m].astype(F32) + core_slots[d, j, m].astype(F32)
                ).astype(BF16)
                if k == 0 and m is xo:
                    diagonal_a(i).start()
                    diagonal_b(i).start()

        each(i, body)

    def second(i):
        def body():
            d = z - OFFSETS[i]
            diagonal_a(i).wait_recv()
            sums2[d, y, xo, :, cut_a] = (
                sums2[d, y, xo, :, cut_a].astype(F32) + a_slots[d].astype(F32)
            ).astype(BF16)
            full_x(i).start()
            diagonal_b(i).wait_recv()
            sums2[d, yo, x, :, cut_b] = (
                sums2[d, yo, x, :, cut_b].astype(F32) + b_slots[d].astype(F32)
            ).astype(BF16)
            full_y(i).start()

        each(i, body)

    def third(i):
        def body():
            d = z - OFFSETS[i]
            full_x(i).wait_recv()
            full_y(i).wait_recv()
            own[d] = (
                sums2[d, y, x].astype(F32) + x_slots2[d].astype(F32) + y_slots2[d].astype(F32)
            ).astype(BF16)

        each(i, body)

    narrow(yo)
    for i in far:
        each(i, lambda i=i: part_copy(i, 0).start())
    for i in far:
        first(i, 0)
    narrow(y)
    for i in far:
        each(i, lambda i=i: part_copy(i, 1).start())
    levels = ((6, 5), (4, 3), (2, 1), (0,))
    for t in range(len(levels) + 2):
        for i in levels[t] if t < len(levels) else ():
            first(i, 1)
        for i in levels[t - 1] if 0 <= t - 1 < len(levels) else ():
            second(i)
        if 0 <= t - 2 < len(levels):
            for i in levels[t - 2]:
                third(i)
            if t - 2 < DEPTH - 1:
                chain_z(place, own, z_slots2, z2_send, z2_recv, whole, order=(DEPTH - 1 - (t - 2),))
    total[...] = hidden[...].astype(F32) + own[z].astype(F32)
    chain_z_end(place, z_slots2, total, z2_send, z2_recv, whole)
    out[...] = total[...].astype(BF16)

    for i in range(CHUNKS):
        x_copy(i).wait_send()
        chain_z_sent(place, sums, z_slots, z_send.at[i], z_recv.at[i], cuts[i])

    def sent(q, i):
        for step in z_steps(i):
            @pl.when(place.has_z(step))
            def _():
                z_copy(q, i, step).wait_send()
        for copy in (x_full(q, i), y_full(q, i), onward(q, i)):
            copy.wait_send()
        for k in range(4):
            core_copy(q, i, k // 2, k % 2).wait_send()

    all_blocks(sent)
    for i in far:
        def body(i=i):
            for copy in (
                part_copy(i, 0), part_copy(i, 1), diagonal_a(i), diagonal_b(i), full_x(i), full_y(i)
            ):
                copy.wait_send()

        each(i, body)
    chain_z_sent(place, own, z_slots2, z2_send, z2_recv, whole)


def local_dense(
    context, out_proj, residual, norm_gain, expert_ids, gates, gate_proj, up_proj, down_proj
):
    group_count = lax.axis_size("group")
    member_count = lax.axis_size("ingroup")
    devices = group_count * member_count
    rows, width = residual.shape
    inner = gate_proj.shape[2]
    expert_total = group_count * (member_count // SLICES)
    capacity = min(rows, max(2, rows * TOPK * 5 // (4 * expert_total)))
    offsets = len(OFFSETS)
    dma = pltpu.SemaphoreType.DMA
    vmem = pl.BlockSpec(memory_space=pltpu.VMEM)
    anywhere = pl.BlockSpec(memory_space=pl.ANY)

    def half(*shape):
        return pltpu.VMEM(shape, BF16)

    return pl.pallas_call(
        functools.partial(layer_kernel, capacity),
        out_shape=jax.ShapeDtypeStruct((rows, width), BF16),
        in_specs=[vmem, anywhere, vmem, vmem, vmem, vmem, anywhere, anywhere, anywhere],
        out_specs=vmem,
        scratch_shapes=[
            half(2, context.shape[1], width // CHUNKS),
            half(width, inner), half(width, inner), half(inner, width),
            half(DEPTH, SIDE, rows, width),
            half(DEPTH, rows, width),
            half(DEPTH, rows, width),
            half(2, DEPTH - 1, rows, width),
            pltpu.VMEM((rows, width), F32),
            half(rows, width),
            half(devices, rows, width + SIDE_COLUMNS),
            half(SIDE, devices * rows // SIDE, inner),
            half(SIDE, 2, DEPTH, SIDE, rows, width),
            half(DEPTH, SIDE, SIDE, rows, width),
            half(DEPTH, SIDE, SIDE, rows, width),
            half(DEPTH, rows, width // 2),
            half(DEPTH, rows, width // 2),
            half(DEPTH, rows, width),
            half(DEPTH, rows, width),
            half(DEPTH, rows, width),
            half(2, DEPTH - 1, rows, width),
            dma((3,)), dma((CHUNKS,)),
            dma((CHUNKS,)), dma((CHUNKS,)),
            dma((CHUNKS, 2, DEPTH - 1)), dma((CHUNKS, 2, DEPTH - 1)),
            dma((PASSES, offsets)), dma((PASSES, offsets)),
            dma((PASSES, offsets, 2)), dma((PASSES, offsets, 2)),
            dma((PASSES, offsets)), dma((PASSES, offsets)),
            dma((PASSES, offsets, 4)), dma((PASSES, offsets, 4)),
            dma((offsets, 2)), dma((offsets, 2)),
            dma((offsets, 2)), dma((offsets, 2)),
            dma((offsets, 2)), dma((offsets, 2)),
            dma((2, DEPTH - 1)), dma((2, DEPTH - 1)),
        ],
        compiler_params=pltpu.CompilerParams(
            collective_id=0, has_side_effects=True, vmem_limit_bytes=58 * 2**20
        ),
        name="layer",
    )(
        context, out_proj, residual, norm_gain.reshape(1, width), expert_ids.T, gates.T, gate_proj,
        up_proj, down_proj,
    )


def solution(mesh):
    in_specs = (
        P("group", "ingroup"),
        P("ingroup", None),
        P(("group", "ingroup"), None),
        P(),
        P(("group", "ingroup"), None),
        P(("group", "ingroup"), None),
        P(("group", "ingroup"), None, None),
        P(("group", "ingroup"), None, None),
        P(("group", "ingroup"), None, None),
    )
    out_specs = P(("group", "ingroup"), None)
    sizes = (mesh.shape["group"], mesh.shape["ingroup"])
    body = local_dense if sizes == (2 * SIDE, SIDE * DEPTH) else local
    return jax.shard_map(body, mesh=mesh, in_specs=in_specs, out_specs=out_specs, check_vma=False)
```

```python
import functools

import jax
import jax.numpy as jnp
from jax import lax
from jax.experimental import pallas as pl
from jax.experimental.pallas import tpu as pltpu
from jax.sharding import PartitionSpec as P

TOPK = 8
SLICES = 4


def slice_output(arrived, gate_block, up_block, down_block):
    shape_in = arrived.shape
    flat_rows = arrived.reshape(-1, shape_in[-1])
    gate_part = jnp.dot(flat_rows, gate_block, preferred_element_type=jnp.float32)
    up_part = jnp.dot(flat_rows, up_block, preferred_element_type=jnp.float32)
    activated = (jax.nn.silu(gate_part) * up_part).astype(jnp.bfloat16)
    partial_out = jnp.dot(activated, down_block, preferred_element_type=jnp.float32).astype(
        jnp.bfloat16
    )
    return partial_out.reshape(shape_in[0], shape_in[1], down_block.shape[1])


def local(context, out_proj, residual, norm_gain, expert_ids, gates, gate_proj, up_proj, down_proj):
    group_count = lax.axis_size("group")
    member_count = lax.axis_size("ingroup")
    rows_here = residual.shape[0]
    model_width = residual.shape[1]
    local_experts = member_count // SLICES
    expert_total = group_count * local_experts
    capacity = min(rows_here, max(2, rows_here * TOPK * 5 // (4 * expert_total)))
    attended = lax.psum_scatter(
        jnp.dot(context, out_proj, preferred_element_type=jnp.float32),
        "ingroup",
        scatter_dimension=0,
        tiled=True,
    )
    hidden = (residual.astype(jnp.float32) + attended).astype(jnp.bfloat16)
    hidden_wide = hidden.astype(jnp.float32)
    inverse = lax.rsqrt(jnp.mean(hidden_wide * hidden_wide, axis=1, keepdims=True) + 1e-06)
    normed = (hidden_wide * inverse * norm_gain).astype(jnp.bfloat16)
    expert_iota = jnp.arange(expert_total, dtype=jnp.int32)
    matches = expert_ids[:, :, None] == expert_iota[None, None, :]
    picked = jnp.any(matches, axis=1)
    weighted = jnp.sum(
        jnp.where(matches, gates.astype(jnp.float32)[:, :, None], jnp.float32(0)), axis=1
    )
    gate_block = gate_proj[0]
    up_block = up_proj[0]
    down_block = down_proj[0]
    capacity_iota = jnp.arange(capacity, dtype=jnp.int32)
    picked_grid = picked.reshape(rows_here, group_count, local_experts)
    touched = jnp.any(picked_grid, axis=2).astype(jnp.int32)
    placed_at = jnp.cumsum(touched, axis=0) - touched
    slot_iota = jnp.arange(rows_here, dtype=jnp.int32)
    selector = (touched.T[:, None, :] > 0) & (placed_at.T[:, None, :] == slot_iota[None, :, None])
    selector_half = selector.astype(jnp.bfloat16)
    outgoing = jnp.einsum(
        "gst,td->gsd", selector_half, normed, preferred_element_type=jnp.float32
    ).astype(jnp.bfloat16)
    gate_grid = weighted.reshape(rows_here, group_count, local_experts).astype(jnp.bfloat16)
    outgoing_gates = jnp.einsum(
        "gst,tgl->gsl", selector_half, gate_grid, preferred_element_type=jnp.float32
    ).astype(jnp.bfloat16)
    arrived_rows, arrived_gates = (
        lax.all_to_all(outgoing, "group", split_axis=0, concat_axis=0, tiled=True),
        lax.all_to_all(outgoing_gates, "group", split_axis=0, concat_axis=0, tiled=True),
    )
    wanted = (arrived_gates > 0).astype(jnp.int32)
    relay_rank = jnp.cumsum(wanted, axis=1) - wanted
    relay_admit = (wanted > 0) & (relay_rank < capacity)
    admit_order = relay_admit.transpose(2, 0, 1)
    rank_order = relay_rank.transpose(2, 0, 1)
    placing = admit_order[:, :, None, :] & (
        rank_order[:, :, None, :] == capacity_iota[None, None, :, None]
    )
    placing_half = placing.astype(jnp.bfloat16)
    expert_rows = jnp.einsum(
        "lgcs,gsd->lgcd", placing_half, arrived_rows, preferred_element_type=jnp.float32
    ).astype(jnp.bfloat16)
    expert_rows = expert_rows.reshape(local_experts, group_count * capacity, model_width)
    dispatch = jnp.broadcast_to(
        expert_rows[:, None], (local_experts, SLICES, group_count * capacity, model_width)
    )
    dispatch = dispatch.reshape(member_count, group_count * capacity, model_width)
    returned = lax.all_to_all(
        slice_output(
            lax.all_to_all(dispatch, "ingroup", split_axis=0, concat_axis=0, tiled=True),
            gate_block,
            up_block,
            down_block,
        ),
        "ingroup",
        split_axis=0,
        concat_axis=0,
        tiled=True,
    )
    returned = returned.reshape(local_experts, SLICES, group_count, capacity, model_width)
    scaled = placing_half * arrived_gates.transpose(2, 0, 1)[:, :, None, :]
    group_out = jnp.einsum("lgcs,lugcd->gsd", scaled, returned, preferred_element_type=jnp.float32)
    back_home = lax.all_to_all(group_out, "group", split_axis=0, concat_axis=0, tiled=True)
    group_iota = jnp.arange(group_count, dtype=jnp.int32)
    fetched = back_home[group_iota[:, None], placed_at.T]
    mixture = jnp.sum(jnp.where(touched.T[:, :, None] > 0, fetched, jnp.float32(0)), axis=0)
    return (hidden_wide + mixture).astype(jnp.bfloat16)


SIDE = 2
DEPTH = 4
CHUNKS = 4
SIDE_COLUMNS = 128
OFFSETS = (0, 1, -1, 2, -2, 3, -3)
MESH = pl.DeviceIdType.MESH
BF16 = jnp.bfloat16
F32 = jnp.float32


class Place:
    def __init__(self):
        group, member = lax.axis_index("group"), lax.axis_index("ingroup")
        self.y, self.c = lax.div(group, 2), lax.rem(group, 2)
        self.z, self.x = lax.div(member, SIDE), lax.rem(member, SIDE)
        self.xo, self.yo, self.co = 1 - self.x, 1 - self.y, 1 - self.c
        self.at_x = {"group": group, "ingroup": self.z * SIDE + self.xo}
        self.at_y = {"group": self.yo * 2 + self.c, "ingroup": member}
        self.at_core = {"group": self.y * 2 + self.co, "ingroup": member}

    def at_z(self, step):
        z = lax.rem(self.z + step + DEPTH, DEPTH)
        return {"group": self.y * 2 + self.c, "ingroup": z * SIDE + self.x}

    def has_z(self, offset):
        return jnp.logical_and(self.z + offset >= 0, self.z + offset < DEPTH)

    def greet(self):
        barrier = pltpu.get_barrier_semaphore()
        for device in (self.at_x, self.at_y, self.at_core, self.at_z(1), self.at_z(-1)):
            pl.semaphore_signal(barrier, inc=1, device_id=device, device_id_type=MESH)

    def meet(self):
        pl.semaphore_wait(pltpu.get_barrier_semaphore(), 5)


def remote(source, target, send, recv, device):
    return pltpu.make_async_remote_copy(
        src_ref=source, dst_ref=target, send_sem=send, recv_sem=recv, device_id=device,
        device_id_type=MESH,
    )


def chain_z(place, sums, slots, send, recv, columns, order=(3, 2, 1)):
    z = place.z
    for k in order:
        for way, step in enumerate((1, -1)):
            @pl.when(place.has_z(step * k))
            def _():
                block = sums.at[z + step * k, :, columns]
                if k < DEPTH - 1:
                    @pl.when(place.has_z(-step))
                    def _():
                        landed = slots.at[way, k, :, columns]
                        remote(landed, landed, send.at[way, k], recv.at[way, k], place.at_z(step)).wait_recv()
                        block[...] = (block[...].astype(F32) + landed[...].astype(F32)).astype(BF16)
                remote(
                    block, slots.at[way, k - 1, :, columns], send.at[way, k - 1], recv.at[way, k - 1],
                    place.at_z(step),
                ).start()


def chain_z_end(place, slots, total, send, recv, columns):
    for way, step in enumerate((1, -1)):
        @pl.when(place.has_z(-step))
        def _():
            landed = slots.at[way, 0, :, columns]
            remote(landed, landed, send.at[way, 0], recv.at[way, 0], place.at_z(step)).wait_recv()
            total[:, columns] += landed[...].astype(F32)


def chain_z_sent(place, sums, slots, send, recv, columns):
    for k in (3, 2, 1):
        for way, step in enumerate((1, -1)):
            @pl.when(place.has_z(step * k))
            def _():
                remote(
                    sums.at[place.z + step * k, :, columns], slots.at[way, k - 1, :, columns],
                    send.at[way, k - 1], recv.at[way, k - 1], place.at_z(step),
                ).wait_send()


def layer_kernel(
    capacity, context, out_proj, residual, gain, ids, gates, gate_proj, up_proj, down_proj, out,
    proj, gate, up, down, part, x_slots, sums, z_slots, total, hidden, rows, act, parts,
    core_slots, sums2, a_slots, b_slots, x_slots2, y_slots2, own, z_slots2,
    w_sem, proj_sem, x_send, x_recv, z_send, z_recv,
    a_send, a_recv, b_send, b_recv, d_send, d_recv, c_send, c_recv,
    core_send, core_recv, e_send, e_recv, f_send, f_recv, z2_send, z2_recv,
):
    place = Place()
    x, y, z, c, xo, yo, co = place.x, place.y, place.z, place.c, place.xo, place.yo, place.co
    rows_here, width = residual.shape
    chunk = width // CHUNKS
    block_rows = rows_here * SIDE * 2 * DEPTH
    cuts = [pl.ds(i * chunk, chunk) for i in range(CHUNKS)]
    extra = pl.ds(width, SIDE_COLUMNS)
    last = CHUNKS - 1
    passes = cuts[:last] + [pl.ds(last * chunk, chunk + SIDE_COLUMNS)]

    def each(i, body):
        pl.when(place.has_z(-OFFSETS[i]))(body)

    def proj_copy(i):
        return pltpu.make_async_copy(out_proj.at[:, cuts[i]], proj.at[i % 2], proj_sem.at[i])

    weight_copies = [
        pltpu.make_async_copy(source.at[0], target, w_sem.at[i])
        for i, (source, target) in enumerate(((gate_proj, gate), (up_proj, up), (down_proj, down)))
    ]
    proj_copy(0).start()
    proj_copy(1).start()
    place.greet()

    def x_copy(i):
        return remote(
            part.at[:, xo, :, cuts[i]], x_slots.at[:, :, cuts[i]], x_send.at[i], x_recv.at[i], place.at_x
        )

    tile = 256
    for i in range(CHUNKS):
        proj_copy(i).wait()

        def multiply(t, carry, i=i):
            inside = pl.ds(pl.multiple_of(t * tile, tile), tile)
            columns = pl.ds(pl.multiple_of(t * tile + i * chunk, tile), tile)
            product = jnp.dot(context[...], proj[i % 2, :, inside], preferred_element_type=F32)
            part[:, :, :, columns] = product.astype(BF16).reshape(DEPTH, SIDE, rows_here, tile)
            return carry

        lax.fori_loop(0, chunk // tile, multiply, 0)
        if i == 0:
            place.meet()
        x_copy(i).start()
        if i + 2 < CHUNKS:
            proj_copy(i + 2).start()
    for copy in weight_copies:
        copy.start()

    lane = lax.broadcasted_iota(jnp.int32, (rows_here, SIDE_COLUMNS), 1)
    down_iota = lax.broadcasted_iota(jnp.int32, (rows_here, rows_here), 0)
    across_iota = lax.broadcasted_iota(jnp.int32, (rows_here, rows_here), 1)

    def upright(line):
        spread = jnp.broadcast_to(line, (rows_here, rows_here))
        return jnp.sum(jnp.where(down_iota == across_iota, spread, 0.0), axis=1, keepdims=True)

    weighted = jnp.zeros((rows_here, SIDE_COLUMNS), F32)
    picked = jnp.zeros((rows_here, SIDE_COLUMNS), F32)
    ids_wide, gates_wide = ids[...].astype(F32), gates[...].astype(F32)
    for j in range(TOPK):
        match = lane.astype(F32) == upright(ids_wide[j : j + 1, :])
        weighted += jnp.where(match, upright(gates_wide[j : j + 1, :]), 0.0)
        picked = jnp.where(match, 1.0, picked)
    before = jnp.where(down_iota > across_iota, 1.0, 0.0).astype(BF16)
    ranking = jnp.dot(before, picked.astype(BF16), preferred_element_type=F32)
    admitted = jnp.where(ranking < capacity, picked, 0.0)
    weighted = jnp.where(admitted > 0.0, weighted, 0.0)

    def head_sum(i):
        x_copy(i).wait_recv()
        for d in range(DEPTH):
            sums[d, :, cuts[i]] = (
                part[d, x, :, cuts[i]].astype(F32) + x_slots[d, :, cuts[i]].astype(F32)
            ).astype(BF16)
        total[:, cuts[i]] = residual[:, cuts[i]].astype(F32) + sums[z, :, cuts[i]].astype(F32)
        chain(i, DEPTH - 1)

    def chain(i, k):
        chain_z(place, sums, z_slots, z_send.at[i], z_recv.at[i], cuts[i], order=(k,))

    def index(y, c, z, x):
        return ((y * 2 + c) * DEPTH + z) * SIDE + x

    mine = index(y, c, z, x)
    squares = []

    def settle(q):
        columns = cuts[q]
        chain_z_end(place, z_slots, total, z_send.at[q], z_recv.at[q], columns)
        rounded = total[:, columns].astype(BF16)
        hidden[:, columns] = rounded
        wide = rounded.astype(F32)
        squares.append(jnp.sum(wide * wide, axis=1, keepdims=True))
        rows[mine, :, columns] = (wide * gain[:, columns]).astype(BF16)
        if q == last:
            inverse = lax.rsqrt(sum(squares) / width + 1e-06)
            high = inverse.astype(BF16).astype(F32)
            side = jnp.where(
                lane == SIDE_COLUMNS - 2, high,
                jnp.where(lane == SIDE_COLUMNS - 1, inverse - high, weighted),
            )
            rows[mine, :, extra] = side.astype(BF16)

    def here(i, by_x, by_y):
        return index(yo if by_y else y, c, z - OFFSETS[i], xo if by_x else x)

    def copy_to(device, block, q, send, recv):
        ref = rows.at[block, :, passes[q]]
        return remote(ref, ref, send, recv, device)

    def z_copy(q, i, step):
        there = OFFSETS.index(OFFSETS[i] + step)
        return copy_to(place.at_z(step), here(i, 0, 0), q, a_send.at[q, there], a_recv.at[q, there])

    def z_steps(i):
        offset = OFFSETS[i]
        return [s for s in (1, -1) if offset * s >= 0 and abs(offset + s) < DEPTH]

    def x_full(q, i, by_x=0):
        return copy_to(place.at_x, here(i, by_x, 0), q, b_send.at[q, i, 0], b_recv.at[q, i, 0])

    def y_full(q, i, by_y=0):
        return copy_to(place.at_y, here(i, 0, by_y), q, b_send.at[q, i, 1], b_recv.at[q, i, 1])

    def route(q):
        return q * 2 // CHUNKS

    def onward(q, i, landed=0):
        device = (place.at_y, place.at_x)[route(q)]
        block = here(i, 1, 1) if landed else here(i, 1 - route(q), route(q))
        return copy_to(device, block, q, d_send.at[q, i], d_recv.at[q, i])

    def core_copy(q, i, by_x, by_y):
        k = by_x * 2 + by_y
        return copy_to(place.at_core, here(i, by_x, by_y), q, c_send.at[q, i, k], c_recv.at[q, i, k])

    def core_wait(q, i, by_x, by_y):
        k = by_x * 2 + by_y
        block = index(yo if by_y else y, co, z - OFFSETS[i], xo if by_x else x)
        copy_to(place.at_core, block, q, c_send.at[q, i, k], c_recv.at[q, i, k]).wait_recv()

    def along_z(q, i):
        def body():
            if i > 0:
                copy_to(place.at_x, here(i, 0, 0), q, a_send.at[q, i], a_recv.at[q, i]).wait_recv()
            for step in z_steps(i):
                @pl.when(place.has_z(step))
                def _():
                    z_copy(q, i, step).start()
            x_full(q, i).start()
            y_full(q, i).start()
            core_copy(q, i, 0, 0).start()

        each(i, body)

    def along_xy(q, i):
        def body():
            arrivals = [(x_full(q, i, 1), (1, 0)), (y_full(q, i, 1), (0, 1))]
            for n in (route(q), 1 - route(q)):
                arrivals[n][0].wait_recv()
                if n == route(q):
                    onward(q, i).start()
                core_copy(q, i, *arrivals[n][1]).start()

        each(i, body)

    def along_diagonal(q, i):
        def body():
            onward(q, i, 1).wait_recv()
            core_copy(q, i, 1, 1).start()

        each(i, body)

    near = ((0,), (1, 2), (3, 4), (5, 6))

    def level(action, q, t):
        if 0 <= t < DEPTH:
            for i in near[t]:
                action(q, i)

    def stage(q, s):
        if s == 0:
            head_sum(q)
        elif s < DEPTH - 1:
            chain(q, DEPTH - 1 - s)
        elif s == DEPTH - 1:
            settle(q)
            level(along_z, q, 0)
        else:
            t = s - (DEPTH - 1)
            level(along_z, q, t)
            level(along_xy, q, t - 1)
            if (q, t - 2) != (last, DEPTH - 1):
                level(along_diagonal, q, t - 2)

    stages = 2 * DEPTH + 1
    for s in range(2 * last + stages):
        for q in range(CHUNKS):
            if 0 <= s - 2 * q < stages:
                stage(q, s - 2 * q)

    def all_blocks(action):
        for q in range(CHUNKS):
            for i in range(len(OFFSETS)):
                each(i, lambda q=q, i=i: action(q, i))

    def cores_near(q, i):
        core_wait(q, i, 0, 0)
        core_wait(q, i, 1, 0)

    def cores_far(q, i):
        core_wait(q, i, 0, 1)
        core_wait(q, i, 1, 1)

    member_count = SIDE * DEPTH
    expert = (y * 2 + c) * (member_count // SLICES) + lax.div(z * SIDE + x, SLICES)
    half_blocks = 2 * DEPTH * SIDE

    def side_of(j):
        side = rows[pl.ds(j * half_blocks, half_blocks), :, extra].reshape(block_rows, SIDE_COLUMNS)
        return side.astype(F32), lax.broadcasted_iota(jnp.int32, (block_rows, SIDE_COLUMNS), 1)

    def widen(j):
        depth = 1024

        def multiply(t, carry):
            columns = pl.ds(pl.multiple_of(t * depth, depth), depth)
            block = rows[pl.ds(j * half_blocks, half_blocks), :, columns].reshape(block_rows, depth)
            return (
                carry[0] + jnp.dot(block, gate[columns, :], preferred_element_type=F32),
                carry[1] + jnp.dot(block, up[columns, :], preferred_element_type=F32),
            )

        zeros = jnp.zeros((block_rows, gate.shape[1]), F32)
        gate_part, up_part = lax.fori_loop(0, width // depth, multiply, (zeros, zeros))
        side, lane = side_of(j)
        inverse = jnp.sum(jnp.where(lane >= SIDE_COLUMNS - 2, side, 0.0), axis=1, keepdims=True)
        gate_part = gate_part * inverse
        act[j] = (gate_part / (1.0 + jnp.exp(-gate_part)) * (up_part * inverse)).astype(BF16)

    def narrow(j):
        side, lane = side_of(j)
        weight = jnp.sum(jnp.where(lane == expert, side, 0.0), axis=1, keepdims=True)
        step = 512

        def multiply(t, carry):
            columns = pl.ds(pl.multiple_of(t * step, step), step)
            product = jnp.dot(act[j], down[:, columns], preferred_element_type=F32) * weight
            parts[j, :, :, :, :, columns] = product.astype(BF16).reshape(
                2, DEPTH, SIDE, rows_here, step
            )
            return carry

        lax.fori_loop(0, width // step, multiply, 0)

    for copy in weight_copies:
        copy.wait()
    all_blocks(cores_near)
    widen(y)
    level(along_diagonal, last, DEPTH - 1)
    all_blocks(cores_far)
    widen(yo)

    half = width // 2
    cut_a, cut_b, whole = pl.ds(0, half), pl.ds(half, half), pl.ds(0, width)
    far = (6, 5, 4, 3, 2, 1, 0)

    def part_copy(i, k):
        d = z - OFFSETS[i]
        j = (yo, y)[k]
        return remote(
            parts.at[j, co, d], core_slots.at[d, j], core_send.at[i, k], core_recv.at[i, k], place.at_core
        )

    def diagonal_a(i):
        d = z - OFFSETS[i]
        return remote(
            sums2.at[d, yo, xo, :, cut_a], a_slots.at[d], e_send.at[i, 0], e_recv.at[i, 0], place.at_y
        )

    def diagonal_b(i):
        d = z - OFFSETS[i]
        return remote(
            sums2.at[d, yo, xo, :, cut_b], b_slots.at[d], e_send.at[i, 1], e_recv.at[i, 1], place.at_x
        )

    def full_x(i):
        d = z - OFFSETS[i]
        return remote(sums2.at[d, y, xo], x_slots2.at[d], f_send.at[i, 0], f_recv.at[i, 0], place.at_x)

    def full_y(i):
        d = z - OFFSETS[i]
        return remote(sums2.at[d, yo, x], y_slots2.at[d], f_send.at[i, 1], f_recv.at[i, 1], place.at_y)

    def first(i, k):
        def body():
            d = z - OFFSETS[i]
            j = (yo, y)[k]
            part_copy(i, k).wait_recv()
            for m in (xo, x):
                sums2[d, j, m] = (
                    parts[j, c, d, m].astype(F32) + core_slots[d, j, m].astype(F32)
                ).astype(BF16)
                if k == 0 and m is xo:
                    diagonal_a(i).start()
                    diagonal_b(i).start()

        each(i, body)

    def second(i):
        def body():
            d = z - OFFSETS[i]
            diagonal_a(i).wait_recv()
            sums2[d, y, xo, :, cut_a] = (
                sums2[d, y, xo, :, cut_a].astype(F32) + a_slots[d].astype(F32)
            ).astype(BF16)
            full_x(i).start()
            diagonal_b(i).wait_recv()
            sums2[d, yo, x, :, cut_b] = (
                sums2[d, yo, x, :, cut_b].astype(F32) + b_slots[d].astype(F32)
            ).astype(BF16)
            full_y(i).start()

        each(i, body)

    def third(i):
        def body():
            d = z - OFFSETS[i]
            full_x(i).wait_recv()
            full_y(i).wait_recv()
            own[d] = (
                sums2[d, y, x].astype(F32) + x_slots2[d].astype(F32) + y_slots2[d].astype(F32)
            ).astype(BF16)

        each(i, body)

    narrow(yo)
    for i in far:
        each(i, lambda i=i: part_copy(i, 0).start())
    for i in far:
        first(i, 0)
    narrow(y)
    for i in far:
        each(i, lambda i=i: part_copy(i, 1).start())
    levels = ((6, 5), (4, 3), (2, 1), (0,))
    for t in range(len(levels) + 2):
        for i in levels[t] if t < len(levels) else ():
            first(i, 1)
        for i in levels[t - 1] if 0 <= t - 1 < len(levels) else ():
            second(i)
        if 0 <= t - 2 < len(levels):
            for i in levels[t - 2]:
                third(i)
            if t - 2 < DEPTH - 1:
                chain_z(place, own, z_slots2, z2_send, z2_recv, whole, order=(DEPTH - 1 - (t - 2),))
    total[...] = hidden[...].astype(F32) + own[z].astype(F32)
    chain_z_end(place, z_slots2, total, z2_send, z2_recv, whole)
    out[...] = total[...].astype(BF16)

    for i in range(CHUNKS):
        x_copy(i).wait_send()
        chain_z_sent(place, sums, z_slots, z_send.at[i], z_recv.at[i], cuts[i])

    def sent(q, i):
        for step in z_steps(i):
            @pl.when(place.has_z(step))
            def _():
                z_copy(q, i, step).wait_send()
        for copy in (x_full(q, i), y_full(q, i), onward(q, i)):
            copy.wait_send()
        for k in range(4):
            core_copy(q, i, k // 2, k % 2).wait_send()

    all_blocks(sent)
    for i in far:
        def body(i=i):
            for copy in (
                part_copy(i, 0), part_copy(i, 1), diagonal_a(i), diagonal_b(i), full_x(i), full_y(i)
            ):
                copy.wait_send()

        each(i, body)
    chain_z_sent(place, own, z_slots2, z2_send, z2_recv, whole)


def local_dense(
    context, out_proj, residual, norm_gain, expert_ids, gates, gate_proj, up_proj, down_proj
):
    group_count = lax.axis_size("group")
    member_count = lax.axis_size("ingroup")
    devices = group_count * member_count
    rows, width = residual.shape
    inner = gate_proj.shape[2]
    expert_total = group_count * (member_count // SLICES)
    capacity = min(rows, max(2, rows * TOPK * 5 // (4 * expert_total)))
    offsets = len(OFFSETS)
    dma = pltpu.SemaphoreType.DMA
    vmem = pl.BlockSpec(memory_space=pltpu.VMEM)
    anywhere = pl.BlockSpec(memory_space=pl.ANY)

    def half(*shape):
        return pltpu.VMEM(shape, BF16)

    return pl.pallas_call(
        functools.partial(layer_kernel, capacity),
        out_shape=jax.ShapeDtypeStruct((rows, width), BF16),
        in_specs=[vmem, anywhere, vmem, vmem, vmem, vmem, anywhere, anywhere, anywhere],
        out_specs=vmem,
        scratch_shapes=[
            half(2, context.shape[1], width // CHUNKS),
            half(width, inner), half(width, inner), half(inner, width),
            half(DEPTH, SIDE, rows, width),
            half(DEPTH, rows, width),
            half(DEPTH, rows, width),
            half(2, DEPTH - 1, rows, width),
            pltpu.VMEM((rows, width), F32),
            half(rows, width),
            half(devices, rows, width + SIDE_COLUMNS),
            half(SIDE, devices * rows // SIDE, inner),
            half(SIDE, 2, DEPTH, SIDE, rows, width),
            half(DEPTH, SIDE, SIDE, rows, width),
            half(DEPTH, SIDE, SIDE, rows, width),
            half(DEPTH, rows, width // 2),
            half(DEPTH, rows, width // 2),
            half(DEPTH, rows, width),
            half(DEPTH, rows, width),
            half(DEPTH, rows, width),
            half(2, DEPTH - 1, rows, width),
            dma((3,)), dma((CHUNKS,)),
            dma((CHUNKS,)), dma((CHUNKS,)),
            dma((CHUNKS, 2, DEPTH - 1)), dma((CHUNKS, 2, DEPTH - 1)),
            dma((CHUNKS, offsets)), dma((CHUNKS, offsets)),
            dma((CHUNKS, offsets, 2)), dma((CHUNKS, offsets, 2)),
            dma((CHUNKS, offsets)), dma((CHUNKS, offsets)),
            dma((CHUNKS, offsets, 4)), dma((CHUNKS, offsets, 4)),
            dma((offsets, 2)), dma((offsets, 2)),
            dma((offsets, 2)), dma((offsets, 2)),
            dma((offsets, 2)), dma((offsets, 2)),
            dma((2, DEPTH - 1)), dma((2, DEPTH - 1)),
        ],
        compiler_params=pltpu.CompilerParams(
            collective_id=0, has_side_effects=True, vmem_limit_bytes=58 * 2**20
        ),
        name="layer",
    )(
        context, out_proj, residual, norm_gain.reshape(1, width), expert_ids.T, gates.T, gate_proj,
        up_proj, down_proj,
    )


def solution(mesh):
    in_specs = (
        P("group", "ingroup"),
        P("ingroup", None),
        P(("group", "ingroup"), None),
        P(),
        P(("group", "ingroup"), None),
        P(("group", "ingroup"), None),
        P(("group", "ingroup"), None, None),
        P(("group", "ingroup"), None, None),
        P(("group", "ingroup"), None, None),
    )
    out_specs = P(("group", "ingroup"), None)
    sizes = (mesh.shape["group"], mesh.shape["ingroup"])
    body = local_dense if sizes == (2 * SIDE, SIDE * DEPTH) else local
    return jax.shard_map(body, mesh=mesh, in_specs=in_specs, out_specs=out_specs, check_vma=False)
```

```python
import functools

import jax
import jax.numpy as jnp
from jax import lax
from jax.experimental import pallas as pl
from jax.experimental.pallas import tpu as pltpu
from jax.sharding import PartitionSpec as P

TOPK = 8
SLICES = 4


def slice_output(arrived, gate_block, up_block, down_block):
    shape_in = arrived.shape
    flat_rows = arrived.reshape(-1, shape_in[-1])
    gate_part = jnp.dot(flat_rows, gate_block, preferred_element_type=jnp.float32)
    up_part = jnp.dot(flat_rows, up_block, preferred_element_type=jnp.float32)
    activated = (jax.nn.silu(gate_part) * up_part).astype(jnp.bfloat16)
    partial_out = jnp.dot(activated, down_block, preferred_element_type=jnp.float32).astype(
        jnp.bfloat16
    )
    return partial_out.reshape(shape_in[0], shape_in[1], down_block.shape[1])


def local(context, out_proj, residual, norm_gain, expert_ids, gates, gate_proj, up_proj, down_proj):
    group_count = lax.axis_size("group")
    member_count = lax.axis_size("ingroup")
    rows_here = residual.shape[0]
    model_width = residual.shape[1]
    local_experts = member_count // SLICES
    expert_total = group_count * local_experts
    capacity = min(rows_here, max(2, rows_here * TOPK * 5 // (4 * expert_total)))
    attended = lax.psum_scatter(
        jnp.dot(context, out_proj, preferred_element_type=jnp.float32),
        "ingroup",
        scatter_dimension=0,
        tiled=True,
    )
    hidden = (residual.astype(jnp.float32) + attended).astype(jnp.bfloat16)
    hidden_wide = hidden.astype(jnp.float32)
    inverse = lax.rsqrt(jnp.mean(hidden_wide * hidden_wide, axis=1, keepdims=True) + 1e-06)
    normed = (hidden_wide * inverse * norm_gain).astype(jnp.bfloat16)
    expert_iota = jnp.arange(expert_total, dtype=jnp.int32)
    matches = expert_ids[:, :, None] == expert_iota[None, None, :]
    picked = jnp.any(matches, axis=1)
    weighted = jnp.sum(
        jnp.where(matches, gates.astype(jnp.float32)[:, :, None], jnp.float32(0)), axis=1
    )
    gate_block = gate_proj[0]
    up_block = up_proj[0]
    down_block = down_proj[0]
    capacity_iota = jnp.arange(capacity, dtype=jnp.int32)
    picked_grid = picked.reshape(rows_here, group_count, local_experts)
    touched = jnp.any(picked_grid, axis=2).astype(jnp.int32)
    placed_at = jnp.cumsum(touched, axis=0) - touched
    slot_iota = jnp.arange(rows_here, dtype=jnp.int32)
    selector = (touched.T[:, None, :] > 0) & (placed_at.T[:, None, :] == slot_iota[None, :, None])
    selector_half = selector.astype(jnp.bfloat16)
    outgoing = jnp.einsum(
        "gst,td->gsd", selector_half, normed, preferred_element_type=jnp.float32
    ).astype(jnp.bfloat16)
    gate_grid = weighted.reshape(rows_here, group_count, local_experts).astype(jnp.bfloat16)
    outgoing_gates = jnp.einsum(
        "gst,tgl->gsl", selector_half, gate_grid, preferred_element_type=jnp.float32
    ).astype(jnp.bfloat16)
    arrived_rows, arrived_gates = (
        lax.all_to_all(outgoing, "group", split_axis=0, concat_axis=0, tiled=True),
        lax.all_to_all(outgoing_gates, "group", split_axis=0, concat_axis=0, tiled=True),
    )
    wanted = (arrived_gates > 0).astype(jnp.int32)
    relay_rank = jnp.cumsum(wanted, axis=1) - wanted
    relay_admit = (wanted > 0) & (relay_rank < capacity)
    admit_order = relay_admit.transpose(2, 0, 1)
    rank_order = relay_rank.transpose(2, 0, 1)
    placing = admit_order[:, :, None, :] & (
        rank_order[:, :, None, :] == capacity_iota[None, None, :, None]
    )
    placing_half = placing.astype(jnp.bfloat16)
    expert_rows = jnp.einsum(
        "lgcs,gsd->lgcd", placing_half, arrived_rows, preferred_element_type=jnp.float32
    ).astype(jnp.bfloat16)
    expert_rows = expert_rows.reshape(local_experts, group_count * capacity, model_width)
    dispatch = jnp.broadcast_to(
        expert_rows[:, None], (local_experts, SLICES, group_count * capacity, model_width)
    )
    dispatch = dispatch.reshape(member_count, group_count * capacity, model_width)
    returned = lax.all_to_all(
        slice_output(
            lax.all_to_all(dispatch, "ingroup", split_axis=0, concat_axis=0, tiled=True),
            gate_block,
            up_block,
            down_block,
        ),
        "ingroup",
        split_axis=0,
        concat_axis=0,
        tiled=True,
    )
    returned = returned.reshape(local_experts, SLICES, group_count, capacity, model_width)
    scaled = placing_half * arrived_gates.transpose(2, 0, 1)[:, :, None, :]
    group_out = jnp.einsum("lgcs,lugcd->gsd", scaled, returned, preferred_element_type=jnp.float32)
    back_home = lax.all_to_all(group_out, "group", split_axis=0, concat_axis=0, tiled=True)
    group_iota = jnp.arange(group_count, dtype=jnp.int32)
    fetched = back_home[group_iota[:, None], placed_at.T]
    mixture = jnp.sum(jnp.where(touched.T[:, :, None] > 0, fetched, jnp.float32(0)), axis=0)
    return (hidden_wide + mixture).astype(jnp.bfloat16)


SIDE = 2
DEPTH = 4
CHUNKS = 4
PASSES = 2
SIDE_COLUMNS = 128
OFFSETS = (0, 1, -1, 2, -2, 3, -3)
MESH = pl.DeviceIdType.MESH
BF16 = jnp.bfloat16
F32 = jnp.float32


class Place:
    def __init__(self):
        group, member = lax.axis_index("group"), lax.axis_index("ingroup")
        self.y, self.c = lax.div(group, 2), lax.rem(group, 2)
        self.z, self.x = lax.div(member, SIDE), lax.rem(member, SIDE)
        self.xo, self.yo, self.co = 1 - self.x, 1 - self.y, 1 - self.c
        self.at_x = {"group": group, "ingroup": self.z * SIDE + self.xo}
        self.at_y = {"group": self.yo * 2 + self.c, "ingroup": member}
        self.at_core = {"group": self.y * 2 + self.co, "ingroup": member}

    def at_z(self, step):
        z = lax.rem(self.z + step + DEPTH, DEPTH)
        return {"group": self.y * 2 + self.c, "ingroup": z * SIDE + self.x}

    def has_z(self, offset):
        return jnp.logical_and(self.z + offset >= 0, self.z + offset < DEPTH)

    def greet(self):
        barrier = pltpu.get_barrier_semaphore()
        for device in (self.at_x, self.at_y, self.at_core, self.at_z(1), self.at_z(-1)):
            pl.semaphore_signal(barrier, inc=1, device_id=device, device_id_type=MESH)

    def meet(self):
        pl.semaphore_wait(pltpu.get_barrier_semaphore(), 5)


def remote(source, target, send, recv, device):
    return pltpu.make_async_remote_copy(
        src_ref=source, dst_ref=target, send_sem=send, recv_sem=recv, device_id=device,
        device_id_type=MESH,
    )


def chain_z(place, sums, slots, send, recv, columns, order=(3, 2, 1)):
    z = place.z
    for k in order:
        for way, step in enumerate((1, -1)):
            @pl.when(place.has_z(step * k))
            def _():
                block = sums.at[z + step * k, :, columns]
                if k < DEPTH - 1:
                    @pl.when(place.has_z(-step))
                    def _():
                        landed = slots.at[way, k, :, columns]
                        remote(landed, landed, send.at[way, k], recv.at[way, k], place.at_z(step)).wait_recv()
                        block[...] = (block[...].astype(F32) + landed[...].astype(F32)).astype(BF16)
                remote(
                    block, slots.at[way, k - 1, :, columns], send.at[way, k - 1], recv.at[way, k - 1],
                    place.at_z(step),
                ).start()


def chain_z_end(place, slots, total, send, recv, columns):
    for way, step in enumerate((1, -1)):
        @pl.when(place.has_z(-step))
        def _():
            landed = slots.at[way, 0, :, columns]
            remote(landed, landed, send.at[way, 0], recv.at[way, 0], place.at_z(step)).wait_recv()
            total[:, columns] += landed[...].astype(F32)


def chain_z_sent(place, sums, slots, send, recv, columns):
    for k in (3, 2, 1):
        for way, step in enumerate((1, -1)):
            @pl.when(place.has_z(step * k))
            def _():
                remote(
                    sums.at[place.z + step * k, :, columns], slots.at[way, k - 1, :, columns],
                    send.at[way, k - 1], recv.at[way, k - 1], place.at_z(step),
                ).wait_send()


def layer_kernel(
    capacity, context, out_proj, residual, gain, ids, gates, gate_proj, up_proj, down_proj, out,
    proj, gate, up, down, part, x_slots, sums, z_slots, total, hidden, rows, act, parts,
    core_slots, sums2, a_slots, b_slots, x_slots2, y_slots2, own, z_slots2,
    w_sem, proj_sem, x_send, x_recv, z_send, z_recv,
    a_send, a_recv, b_send, b_recv, d_send, d_recv, c_send, c_recv,
    core_send, core_recv, e_send, e_recv, f_send, f_recv, z2_send, z2_recv,
):
    place = Place()
    x, y, z, c, xo, yo, co = place.x, place.y, place.z, place.c, place.xo, place.yo, place.co
    rows_here, width = residual.shape
    chunk = width // CHUNKS
    span = width // PASSES
    block_rows = rows_here * SIDE * 2 * DEPTH
    cuts = [pl.ds(i * chunk, chunk) for i in range(CHUNKS)]
    extra = pl.ds(width, SIDE_COLUMNS)
    passes = [pl.ds(0, span), pl.ds(span, span + SIDE_COLUMNS)]

    def each(i, body):
        pl.when(place.has_z(-OFFSETS[i]))(body)

    def proj_copy(i):
        return pltpu.make_async_copy(out_proj.at[:, cuts[i]], proj.at[i % 2], proj_sem.at[i])

    weight_copies = [
        pltpu.make_async_copy(source.at[0], target, w_sem.at[i])
        for i, (source, target) in enumerate(((gate_proj, gate), (up_proj, up), (down_proj, down)))
    ]
    proj_copy(0).start()
    proj_copy(1).start()
    place.greet()

    def x_copy(i):
        return remote(
            part.at[:, xo, :, cuts[i]], x_slots.at[:, :, cuts[i]], x_send.at[i], x_recv.at[i], place.at_x
        )

    tile = 256
    for i in range(CHUNKS):
        proj_copy(i).wait()

        def multiply(t, carry, i=i):
            inside = pl.ds(pl.multiple_of(t * tile, tile), tile)
            columns = pl.ds(pl.multiple_of(t * tile + i * chunk, tile), tile)
            product = jnp.dot(context[...], proj[i % 2, :, inside], preferred_element_type=F32)
            part[:, :, :, columns] = product.astype(BF16).reshape(DEPTH, SIDE, rows_here, tile)
            return carry

        lax.fori_loop(0, chunk // tile, multiply, 0)
        if i == 0:
            place.meet()
        x_copy(i).start()
        if i + 2 < CHUNKS:
            proj_copy(i + 2).start()
    for copy in weight_copies:
        copy.start()

    lane = lax.broadcasted_iota(jnp.int32, (rows_here, SIDE_COLUMNS), 1)
    down_iota = lax.broadcasted_iota(jnp.int32, (rows_here, rows_here), 0)
    across_iota = lax.broadcasted_iota(jnp.int32, (rows_here, rows_here), 1)

    def upright(line):
        spread = jnp.broadcast_to(line, (rows_here, rows_here))
        return jnp.sum(jnp.where(down_iota == across_iota, spread, 0.0), axis=1, keepdims=True)

    weighted = jnp.zeros((rows_here, SIDE_COLUMNS), F32)
    picked = jnp.zeros((rows_here, SIDE_COLUMNS), F32)
    ids_wide, gates_wide = ids[...].astype(F32), gates[...].astype(F32)
    for j in range(TOPK):
        match = lane.astype(F32) == upright(ids_wide[j : j + 1, :])
        weighted += jnp.where(match, upright(gates_wide[j : j + 1, :]), 0.0)
        picked = jnp.where(match, 1.0, picked)
    before = jnp.where(down_iota > across_iota, 1.0, 0.0).astype(BF16)
    ranking = jnp.dot(before, picked.astype(BF16), preferred_element_type=F32)
    admitted = jnp.where(ranking < capacity, picked, 0.0)
    weighted = jnp.where(admitted > 0.0, weighted, 0.0)

    def head_sum(i):
        x_copy(i).wait_recv()
        for d in range(DEPTH):
            sums[d, :, cuts[i]] = (
                part[d, x, :, cuts[i]].astype(F32) + x_slots[d, :, cuts[i]].astype(F32)
            ).astype(BF16)
        total[:, cuts[i]] = residual[:, cuts[i]].astype(F32) + sums[z, :, cuts[i]].astype(F32)
        chain(i, 3)

    def chain(i, k):
        chain_z(place, sums, z_slots, z_send.at[i], z_recv.at[i], cuts[i], order=(k,))

    def index(y, c, z, x):
        return ((y * 2 + c) * DEPTH + z) * SIDE + x

    mine = index(y, c, z, x)
    squares = []

    def settle(q):
        per = CHUNKS // PASSES
        for i in range(q * per, (q + 1) * per):
            chain_z_end(place, z_slots, total, z_send.at[i], z_recv.at[i], cuts[i])
        columns = pl.ds(q * span, span)
        rounded = total[:, columns].astype(BF16)
        hidden[:, columns] = rounded
        wide = rounded.astype(F32)
        squares.append(jnp.sum(wide * wide, axis=1, keepdims=True))
        rows[mine, :, columns] = (wide * gain[:, columns]).astype(BF16)
        if q == PASSES - 1:
            inverse = lax.rsqrt(sum(squares) / width + 1e-06)
            high = inverse.astype(BF16).astype(F32)
            side = jnp.where(
                lane == SIDE_COLUMNS - 2, high,
                jnp.where(lane == SIDE_COLUMNS - 1, inverse - high, weighted),
            )
            rows[mine, :, extra] = side.astype(BF16)

    def here(i, by_x, by_y):
        return index(yo if by_y else y, c, z - OFFSETS[i], xo if by_x else x)

    def copy_to(device, block, q, send, recv):
        ref = rows.at[block, :, passes[q]]
        return remote(ref, ref, send, recv, device)

    def z_copy(q, i, step):
        there = OFFSETS.index(OFFSETS[i] + step)
        return copy_to(place.at_z(step), here(i, 0, 0), q, a_send.at[q, there], a_recv.at[q, there])

    def z_steps(i):
        offset = OFFSETS[i]
        return [s for s in (1, -1) if offset * s >= 0 and abs(offset + s) < DEPTH]

    def x_full(q, i, by_x=0):
        return copy_to(place.at_x, here(i, by_x, 0), q, b_send.at[q, i, 0], b_recv.at[q, i, 0])

    def y_full(q, i, by_y=0):
        return copy_to(place.at_y, here(i, 0, by_y), q, b_send.at[q, i, 1], b_recv.at[q, i, 1])

    def onward(q, i, landed=0):
        device = (place.at_y, place.at_x)[q]
        block = here(i, 1, 1) if landed else here(i, 1 - q, q)
        return copy_to(device, block, q, d_send.at[q, i], d_recv.at[q, i])

    def core_copy(q, i, by_y, owner):
        pair = pl.ds(index(yo if by_y else y, owner, z - OFFSETS[i], 0), SIDE)
        return copy_to(place.at_core, pair, q, c_send.at[q, i, by_y], c_recv.at[q, i, by_y])

    def along_z(q, i):
        def body():
            if i > 0:
                copy_to(place.at_x, here(i, 0, 0), q, a_send.at[q, i], a_recv.at[q, i]).wait_recv()
            for step in z_steps(i):
                @pl.when(place.has_z(step))
                def _():
                    z_copy(q, i, step).start()
            x_full(q, i).start()
            y_full(q, i).start()

        each(i, body)

    def along_xy(q, i):
        def body():
            arrivals = (x_full(q, i, 1), y_full(q, i, 1))
            arrivals[q].wait_recv()
            onward(q, i).start()
            arrivals[1 - q].wait_recv()
            core_copy(q, i, 0, c).start()

        each(i, body)

    def along_diagonal(q, i):
        def body():
            onward(q, i, 1).wait_recv()
            core_copy(q, i, 1, c).start()

        each(i, body)

    near = ((0,), (1, 2), (3, 4), (5, 6))

    def level(action, q, t):
        if 0 <= t < DEPTH:
            for i in near[t]:
                action(q, i)

    head_sum(0)
    chain(0, 2)
    head_sum(1)
    chain(0, 1)
    chain(1, 2)
    head_sum(2)
    chain(1, 1)
    chain(2, 2)
    settle(0)
    level(along_z, 0, 0)
    head_sum(3)
    chain(2, 1)
    chain(3, 2)
    level(along_z, 0, 1)
    level(along_xy, 0, 0)
    chain(3, 1)
    settle(1)
    for t in range(DEPTH + 1):
        level(along_z, 1, t)
        level(along_z, 0, t + 2)
        level(along_xy, 0, t + 1)
        level(along_xy, 1, t - 1)
        level(along_diagonal, 0, t)
        level(along_diagonal, 1, t - 2)

    def all_blocks(action):
        for q in range(PASSES):
            for i in range(len(OFFSETS)):
                each(i, lambda q=q, i=i: action(q, i))

    def cores_near(q, i):
        core_copy(q, i, 0, co).wait_recv()

    def cores_far(q, i):
        core_copy(q, i, 1, co).wait_recv()

    member_count = SIDE * DEPTH
    expert = (y * 2 + c) * (member_count // SLICES) + lax.div(z * SIDE + x, SLICES)
    half_blocks = 2 * DEPTH * SIDE

    def side_of(j):
        side = rows[pl.ds(j * half_blocks, half_blocks), :, extra].reshape(block_rows, SIDE_COLUMNS)
        return side.astype(F32), lax.broadcasted_iota(jnp.int32, (block_rows, SIDE_COLUMNS), 1)

    def widen(j):
        depth = 1024

        def multiply(t, carry):
            columns = pl.ds(pl.multiple_of(t * depth, depth), depth)
            block = rows[pl.ds(j * half_blocks, half_blocks), :, columns].reshape(block_rows, depth)
            return (
                carry[0] + jnp.dot(block, gate[columns, :], preferred_element_type=F32),
                carry[1] + jnp.dot(block, up[columns, :], preferred_element_type=F32),
            )

        zeros = jnp.zeros((block_rows, gate.shape[1]), F32)
        gate_part, up_part = lax.fori_loop(0, width // depth, multiply, (zeros, zeros))
        side, lane = side_of(j)
        inverse = jnp.sum(jnp.where(lane >= SIDE_COLUMNS - 2, side, 0.0), axis=1, keepdims=True)
        gate_part = gate_part * inverse
        act[j] = (gate_part / (1.0 + jnp.exp(-gate_part)) * (up_part * inverse)).astype(BF16)

    def narrow(j):
        side, lane = side_of(j)
        weight = jnp.sum(jnp.where(lane == expert, side, 0.0), axis=1, keepdims=True)
        step = 512

        def multiply(t, carry):
            columns = pl.ds(pl.multiple_of(t * step, step), step)
            product = jnp.dot(act[j], down[:, columns], preferred_element_type=F32) * weight
            parts[j, :, :, :, :, columns] = product.astype(BF16).reshape(
                2, DEPTH, SIDE, rows_here, step
            )
            return carry

        lax.fori_loop(0, width // step, multiply, 0)

    for copy in weight_copies:
        copy.wait()
    all_blocks(cores_near)
    widen(y)
    level(along_diagonal, 1, DEPTH - 1)
    all_blocks(cores_far)
    widen(yo)

    half = width // 2
    cut_a, cut_b, whole = pl.ds(0, half), pl.ds(half, half), pl.ds(0, width)
    far = (6, 5, 4, 3, 2, 1, 0)

    def part_copy(i, k):
        d = z - OFFSETS[i]
        j = (yo, y)[k]
        return remote(
            parts.at[j, co, d], core_slots.at[d, j], core_send.at[i, k], core_recv.at[i, k], place.at_core
        )

    def diagonal_a(i):
        d = z - OFFSETS[i]
        return remote(
            sums2.at[d, yo, xo, :, cut_a], a_slots.at[d], e_send.at[i, 0], e_recv.at[i, 0], place.at_y
        )

    def diagonal_b(i):
        d = z - OFFSETS[i]
        return remote(
            sums2.at[d, yo, xo, :, cut_b], b_slots.at[d], e_send.at[i, 1], e_recv.at[i, 1], place.at_x
        )

    def full_x(i):
        d = z - OFFSETS[i]
        return remote(sums2.at[d, y, xo], x_slots2.at[d], f_send.at[i, 0], f_recv.at[i, 0], place.at_x)

    def full_y(i):
        d = z - OFFSETS[i]
        return remote(sums2.at[d, yo, x], y_slots2.at[d], f_send.at[i, 1], f_recv.at[i, 1], place.at_y)

    def first(i, k):
        def body():
            d = z - OFFSETS[i]
            j = (yo, y)[k]
            part_copy(i, k).wait_recv()
            for m in (xo, x):
                sums2[d, j, m] = (
                    parts[j, c, d, m].astype(F32) + core_slots[d, j, m].astype(F32)
                ).astype(BF16)
                if k == 0 and m is xo:
                    diagonal_a(i).start()
                    diagonal_b(i).start()

        each(i, body)

    def second(i):
        def body():
            d = z - OFFSETS[i]
            diagonal_a(i).wait_recv()
            sums2[d, y, xo, :, cut_a] = (
                sums2[d, y, xo, :, cut_a].astype(F32) + a_slots[d].astype(F32)
            ).astype(BF16)
            full_x(i).start()
            diagonal_b(i).wait_recv()
            sums2[d, yo, x, :, cut_b] = (
                sums2[d, yo, x, :, cut_b].astype(F32) + b_slots[d].astype(F32)
            ).astype(BF16)
            full_y(i).start()

        each(i, body)

    def third(i):
        def body():
            d = z - OFFSETS[i]
            full_x(i).wait_recv()
            full_y(i).wait_recv()
            own[d] = (
                sums2[d, y, x].astype(F32) + x_slots2[d].astype(F32) + y_slots2[d].astype(F32)
            ).astype(BF16)

        each(i, body)

    narrow(yo)
    for i in far:
        each(i, lambda i=i: part_copy(i, 0).start())
    for i in far:
        first(i, 0)
    narrow(y)
    for i in far:
        each(i, lambda i=i: part_copy(i, 1).start())
    levels = ((6, 5), (4, 3), (2, 1), (0,))
    for t in range(len(levels) + 2):
        for i in levels[t] if t < len(levels) else ():
            first(i, 1)
        for i in levels[t - 1] if 0 <= t - 1 < len(levels) else ():
            second(i)
        if 0 <= t - 2 < len(levels):
            for i in levels[t - 2]:
                third(i)
            if t - 2 < DEPTH - 1:
                chain_z(place, own, z_slots2, z2_send, z2_recv, whole, order=(DEPTH - 1 - (t - 2),))
    total[...] = hidden[...].astype(F32) + own[z].astype(F32)
    chain_z_end(place, z_slots2, total, z2_send, z2_recv, whole)
    out[...] = total[...].astype(BF16)

    for i in range(CHUNKS):
        x_copy(i).wait_send()
        chain_z_sent(place, sums, z_slots, z_send.at[i], z_recv.at[i], cuts[i])

    def sent(q, i):
        for step in z_steps(i):
            @pl.when(place.has_z(step))
            def _():
                z_copy(q, i, step).wait_send()
        for copy in (x_full(q, i), y_full(q, i), onward(q, i)):
            copy.wait_send()
        for by_y in (0, 1):
            core_copy(q, i, by_y, c).wait_send()

    all_blocks(sent)
    for i in far:
        def body(i=i):
            for copy in (
                part_copy(i, 0), part_copy(i, 1), diagonal_a(i), diagonal_b(i), full_x(i), full_y(i)
            ):
                copy.wait_send()

        each(i, body)
    chain_z_sent(place, own, z_slots2, z2_send, z2_recv, whole)


def local_dense(
    context, out_proj, residual, norm_gain, expert_ids, gates, gate_proj, up_proj, down_proj
):
    group_count = lax.axis_size("group")
    member_count = lax.axis_size("ingroup")
    devices = group_count * member_count
    rows, width = residual.shape
    inner = gate_proj.shape[2]
    expert_total = group_count * (member_count // SLICES)
    capacity = min(rows, max(2, rows * TOPK * 5 // (4 * expert_total)))
    offsets = len(OFFSETS)
    dma = pltpu.SemaphoreType.DMA
    vmem = pl.BlockSpec(memory_space=pltpu.VMEM)
    anywhere = pl.BlockSpec(memory_space=pl.ANY)

    def half(*shape):
        return pltpu.VMEM(shape, BF16)

    return pl.pallas_call(
        functools.partial(layer_kernel, capacity),
        out_shape=jax.ShapeDtypeStruct((rows, width), BF16),
        in_specs=[vmem, anywhere, vmem, vmem, vmem, vmem, anywhere, anywhere, anywhere],
        out_specs=vmem,
        scratch_shapes=[
            half(2, context.shape[1], width // CHUNKS),
            half(width, inner), half(width, inner), half(inner, width),
            half(DEPTH, SIDE, rows, width),
            half(DEPTH, rows, width),
            half(DEPTH, rows, width),
            half(2, DEPTH - 1, rows, width),
            pltpu.VMEM((rows, width), F32),
            half(rows, width),
            half(devices, rows, width + SIDE_COLUMNS),
            half(SIDE, devices * rows // SIDE, inner),
            half(SIDE, 2, DEPTH, SIDE, rows, width),
            half(DEPTH, SIDE, SIDE, rows, width),
            half(DEPTH, SIDE, SIDE, rows, width),
            half(DEPTH, rows, width // 2),
            half(DEPTH, rows, width // 2),
            half(DEPTH, rows, width),
            half(DEPTH, rows, width),
            half(DEPTH, rows, width),
            half(2, DEPTH - 1, rows, width),
            dma((3,)), dma((CHUNKS,)),
            dma((CHUNKS,)), dma((CHUNKS,)),
            dma((CHUNKS, 2, DEPTH - 1)), dma((CHUNKS, 2, DEPTH - 1)),
            dma((PASSES, offsets)), dma((PASSES, offsets)),
            dma((PASSES, offsets, 2)), dma((PASSES, offsets, 2)),
            dma((PASSES, offsets)), dma((PASSES, offsets)),
            dma((PASSES, offsets, 2)), dma((PASSES, offsets, 2)),
            dma((offsets, 2)), dma((offsets, 2)),
            dma((offsets, 2)), dma((offsets, 2)),
            dma((offsets, 2)), dma((offsets, 2)),
            dma((2, DEPTH - 1)), dma((2, DEPTH - 1)),
        ],
        compiler_params=pltpu.CompilerParams(
            collective_id=0, has_side_effects=True, vmem_limit_bytes=58 * 2**20
        ),
        name="layer",
    )(
        context, out_proj, residual, norm_gain.reshape(1, width), expert_ids.T, gates.T, gate_proj,
        up_proj, down_proj,
    )


def solution(mesh):
    in_specs = (
        P("group", "ingroup"),
        P("ingroup", None),
        P(("group", "ingroup"), None),
        P(),
        P(("group", "ingroup"), None),
        P(("group", "ingroup"), None),
        P(("group", "ingroup"), None, None),
        P(("group", "ingroup"), None, None),
        P(("group", "ingroup"), None, None),
    )
    out_specs = P(("group", "ingroup"), None)
    sizes = (mesh.shape["group"], mesh.shape["ingroup"])
    body = local_dense if sizes == (2 * SIDE, SIDE * DEPTH) else local
    return jax.shard_map(body, mesh=mesh, in_specs=in_specs, out_specs=out_specs, check_vma=False)
```
